512 devices in a mesh: dp: 16 (over z), mp: 32 (over x, y, core).
Axes of the slice: x: 4, y: 4, z: 16, core: 2. Of those that a mesh axis runs over, the one named last changes fastest.
Arguments:
- activations: bfloat16 [8192, 8192], P('dp', 'mp'), may hold values from -6 to 6
- out_grads: bfloat16 [8192, 29568], P('dp', 'mp'), may hold values from -0.5 to 0.5
- test_matrix: bfloat16 [29568, 512], P('mp'), may hold values from -0.03125 to 0.03125
- first_moment: float32 [512, 29568], P('dp', 'mp'), may hold values from -12 to 12
- second_moment: float32 [512, 29568], P('dp', 'mp'), may hold values from 0.01 to 0.1
Outputs:
- update: bfloat16 [32, 256, 29568], P(None, 'dp', 'mp')
- new_first: float32 [512, 29568], P('dp', 'mp')
- new_second: float32 [512, 29568], P('dp', 'mp')
The draws below stay inside these ranges and needn't reach their ends.
All inputs are finite; a program needn't handle non-finite values.
Results may differ from the reference program's by a relative error of at most 0.013.
Values may be sent and summed in bfloat16 or wider, within the bound.
A program may use at most 64 MiB of HBM per device.

```python
import math
import jax
import jax.numpy as jnp
from jax import lax

D = 8192
FF = 29568
R = 512
STEP = 100
TOK_DEV = 512
TOKENS = 8192
N_MP = 32


def draw_first_moment(key, part):
    key = jax.random.fold_in(key, 11)
    rank_pos = jnp.arange(R, dtype=jnp.float32)[:, None] / R
    column_pos = jnp.arange(FF, dtype=jnp.float32)[None, :] / FF
    base = jax.random.truncated_normal(key, -4.0, 4.0, (R, FF), jnp.float32)
    spread = 0.5
    return 0.3 * base * 10.0 ** (spread * (rank_pos + column_pos))


def draw_activations(key, part):
    key = jax.random.fold_in(key, 23)
    base_key = jax.random.fold_in(key, 1)
    factor_key = jax.random.fold_in(key, 2)
    feature_pos = jnp.arange(D, dtype=jnp.float32)[None, :] / D
    rough = jax.random.uniform(factor_key, (1, D), jnp.float32, 0.5, 1.5)
    base = jax.random.truncated_normal(base_key, -4.0, 4.0, (TOKENS, D), jnp.float32)
    spread = 1.5
    return (base * rough * 10.0 ** (spread * (feature_pos - 1.0))).astype(jnp.bfloat16)


def steps_of(stream_key, shape, pieces, low, largest):
    gain = 1.0
    for position, blocks in pieces:
        steps = jax.random.uniform(jax.random.fold_in(jax.random.fold_in(stream_key, 6), position), (blocks,), jnp.float32, low / len(pieces), largest / len(pieces))
        gain = gain * jnp.repeat(jnp.exp(steps), shape[position] // blocks).reshape((-1,) + (1,) * (len(shape) - 1 - position))
    return gain


def bell_draw(stream_key, extent, width, most, pieces=(), kind=jnp.bfloat16):
    entries = jax.random.normal(stream_key, extent, jnp.float32) * width
    if len(pieces) > 0:
        entries = steps_of(stream_key, extent, pieces, -0.22, 0.18) * entries
    return jnp.clip(entries, min=-most, max=most).astype(kind)


def setup_inputs(seed: int = 0) -> dict:
    key_list = jax.random.split(jax.random.key(seed), 6)
    return {
        "activations": draw_activations(jax.random.fold_in(key_list[5], 71), 0),
        "out_grads": bell_draw(key_list[1], (TOKENS, FF), (TOK_DEV // 4) ** -0.5, 0.5, ((0, 16), (1, 32))),
        "test_matrix": bell_draw(key_list[2], (FF, R), FF ** -0.5, 0.03125, ((0, 32),)),
        "first_moment": draw_first_moment(jax.random.fold_in(key_list[5], 71), 0),
        "second_moment": jnp.clip(jnp.exp(math.log(0.1) - 2.3025851 * jax.random.uniform(key_list[4], (R, FF), jnp.float32) ** steps_of(key_list[4], (R, FF), ((0, 16), (1, 32)), -0.2, 0.2)), 0.01, 0.1),
    }


beta_one = 0.9
beta_two = 0.999
adam_eps = 1e-08
norm_eps = 1e-06

def reference(activations, out_grads, test_matrix, first_moment, second_moment):
    sketch_in = jnp.dot(out_grads.astype(jnp.float32), test_matrix.astype(jnp.float32), preferred_element_type=jnp.float32).astype(jnp.bfloat16)
    sketch = jnp.dot(activations.T.astype(jnp.float32), sketch_in.astype(jnp.float32), preferred_element_type=jnp.float32)
    gram_matrix = jnp.dot(sketch.T.astype(jnp.float32), sketch.astype(jnp.float32), precision=lax.Precision.HIGHEST, preferred_element_type=jnp.float32)
    lower_factor = jnp.linalg.cholesky(gram_matrix)
    basis = lax.linalg.triangular_solve(lower_factor, sketch, left_side=False, lower=True, transpose_a=True)
    basis_b = basis.astype(jnp.bfloat16)
    coords = jnp.dot(activations.astype(jnp.float32), basis_b.astype(jnp.float32), preferred_element_type=jnp.float32).astype(jnp.bfloat16)
    projected = jnp.dot(coords.T.astype(jnp.float32), out_grads.astype(jnp.float32), preferred_element_type=jnp.float32)
    new_first = beta_one * first_moment + (1.0 - beta_one) * projected
    new_second = beta_two * second_moment + (1.0 - beta_two) * projected * projected
    correct_one = 1.0 - beta_one ** STEP
    correct_two = 1.0 - beta_two ** STEP
    direction = new_first / correct_one / (jnp.sqrt(new_second / correct_two) + adam_eps)
    factor = lax.rsqrt(jnp.mean(direction * direction) + norm_eps)
    direction_b = direction.astype(jnp.bfloat16)
    product = jnp.dot(basis_b.astype(jnp.float32), direction_b.astype(jnp.float32), preferred_element_type=jnp.float32)
    update = (factor * product).astype(jnp.bfloat16).reshape(N_MP, D // N_MP, FF)
    return (update, new_first, new_second)
```

```python
import jax
import jax.numpy as jnp
from jax import lax
from jax.experimental import pallas as pl
from jax.experimental.pallas import tpu as pltpu
from jax.sharding import PartitionSpec as P

FF = 29568
R = 512
STEP = 100

beta_one = 0.9
beta_two = 0.999
adam_eps = 1e-08
norm_eps = 1e-06

MESH = pl.DeviceIdType.MESH
F32 = jnp.float32
BF16 = jnp.bfloat16
CHIPS = 16
DP = 16


def place():
    mp = lax.axis_index("mp")
    core = mp % 2
    chip = mp // 2
    return lax.axis_index("dp"), mp, chip, core


def chip_at(chip, k):
    x = (chip // 4 + k // 4) % 4
    y = (chip % 4 + k % 4) % 4
    return x * 4 + y


def greet(dp_offsets):
    dp, mp, chip, core = place()
    barrier = pltpu.get_barrier_semaphore()
    pl.semaphore_signal(barrier, inc=1, device_id={"mp": chip * 2 + 1 - core}, device_id_type=MESH)

    def to_chip(k, _):
        pl.semaphore_signal(
            barrier, inc=1, device_id={"mp": chip_at(chip, k) * 2 + core}, device_id_type=MESH
        )
        return 0

    lax.fori_loop(1, CHIPS, to_chip, 0)

    def to_ring(k, _):
        pl.semaphore_signal(barrier, inc=1, device_id={"dp": (dp + k) % DP}, device_id_type=MESH)
        return 0

    if dp_offsets == "all":
        lax.fori_loop(1, DP, to_ring, 0)
        return barrier, 1 + (CHIPS - 1) + (DP - 1)
    to_ring(1, 0)
    to_ring(DP - 1, 0)
    return barrier, 1 + (CHIPS - 1) + 2


def send(src, dst, sends, recvs, where):
    return pltpu.make_async_remote_copy(
        src_ref=src, dst_ref=dst, send_sem=sends, recv_sem=recvs, device_id=where, device_id_type=MESH
    )


def plane_scatter(stage, landed, sends, recvs):
    _, _, chip, core = place()

    def copy(k):
        there = chip_at(chip, k)
        return send(
            stage.at[there], landed.at[k - 1], sends.at[k - 1], recvs.at[k - 1], {"mp": there * 2 + core}
        )

    def go(k, _):
        copy(k).start()
        return 0

    lax.fori_loop(1, CHIPS, go, 0)
    return copy


def plane_gather(block, sends, recvs):
    _, _, chip, core = place()

    def copy(k):
        there = chip_at(chip, k)
        return send(block, block, sends.at[k - 1], recvs.at[k - 1], {"mp": there * 2 + core})

    def go(k, _):
        copy(k).start()
        return 0

    lax.fori_loop(1, CHIPS, go, 0)
    return copy


def wait_all(copy, first, last, recv=True):
    def step(k, _):
        if recv:
            copy(k).wait_recv()
        else:
            copy(k).wait_send()
        return 0

    lax.fori_loop(first, last, step, 0)


class PlaneSum:
    def scratch(kind):
        return [
            pltpu.VMEM((256, R), kind),
            pltpu.VMEM((256, R), kind),
            pltpu.VMEM((CHIPS, 16, R), kind),
            pltpu.VMEM((CHIPS - 1, 16, R), kind),
            pltpu.SemaphoreType.DMA((4,)),
            pltpu.SemaphoreType.DMA((CHIPS - 1,)),
            pltpu.SemaphoreType.DMA((CHIPS - 1,)),
            pltpu.SemaphoreType.DMA((CHIPS - 1,)),
            pltpu.SemaphoreType.DMA((CHIPS - 1,)),
        ]

    def run(half_of, full, kind, refs, between=None):
        give, take, stage, landed, pair_sems, s1, r1, s2, r2 = refs
        dp, mp, chip, core = place()
        partner = {"mp": chip * 2 + 1 - core}
        give[...] = half_of(1 - core).astype(kind)
        swap = send(give, take, pair_sems.at[0], pair_sems.at[1], partner)
        swap.start()
        own = half_of(core)
        swap.wait_recv()
        stage[...] = (own + take[...].astype(F32)).astype(kind).reshape(CHIPS, 16, R)
        scatter = plane_scatter(stage, landed, s1, r1)

        def add(k, total):
            scatter(k).wait_recv()
            return total + landed[k - 1].astype(F32)

        total = lax.fori_loop(1, CHIPS, add, stage[chip].astype(F32))
        mine = pl.ds(pl.multiple_of(core * 256 + chip * 16, 16), 16)
        full[mine, :] = total.astype(kind)
        gather = plane_gather(full.at[mine, :], s2, r2)
        wait_all(gather, 1, CHIPS)
        half = full.at[pl.ds(pl.multiple_of(core * 256, 256), 256), :]
        swap_full = send(half, half, pair_sems.at[2], pair_sems.at[3], partner)
        swap_full.start()
        if between is not None:
            between()
        swap_full.wait_recv()

        def finish():
            swap.wait_send()
            wait_all(scatter, 1, CHIPS, recv=False)
            wait_all(gather, 1, CHIPS, recv=False)
            swap_full.wait_send()

        return finish


class Ring:
    RIGHT, LEFT = 8, 7

    def scratch_scatter(rows, width, parts):
        return [
            pltpu.VMEM((Ring.RIGHT, rows, width), BF16),
            pltpu.VMEM((Ring.RIGHT, rows, width), BF16),
            pltpu.VMEM((Ring.LEFT, rows, width), BF16),
            pltpu.VMEM((Ring.LEFT, rows, width), BF16),
            pltpu.SemaphoreType.DMA((Ring.RIGHT, parts)),
            pltpu.SemaphoreType.DMA((Ring.RIGHT, parts)),
            pltpu.SemaphoreType.DMA((Ring.LEFT, parts)),
            pltpu.SemaphoreType.DMA((Ring.LEFT, parts)),
        ]

    def scratch_gather(parts):
        return [
            pltpu.SemaphoreType.DMA((Ring.RIGHT, parts)),
            pltpu.SemaphoreType.DMA((Ring.RIGHT, parts)),
            pltpu.SemaphoreType.DMA((Ring.LEFT, parts)),
            pltpu.SemaphoreType.DMA((Ring.LEFT, parts)),
        ]

    def reduce_scatter(local, refs, rows, parts, put):
        give_r, take_r, give_l, take_l, sr, rr, sl, rl = refs
        dp, _, _, _ = place()
        right, left = {"dp": (dp + 1) % DP}, {"dp": (dp + DP - 1) % DP}
        piece = rows // parts

        def cut(p):
            return pl.ds(p * piece, piece)

        def copy_r(s, p):
            return send(
                give_r.at[s, cut(p)], take_r.at[s, cut(p)], sr.at[s, p], rr.at[s, p], right
            )

        def copy_l(s, p):
            return send(
                give_l.at[s, cut(p)], take_l.at[s, cut(p)], sl.at[s, p], rl.at[s, p], left
            )

        for p in range(parts):
            give_r[0, cut(p)] = local[(dp + 8) % DP, cut(p)].astype(BF16)
            copy_r(0, p).start()
            give_l[0, cut(p)] = local[(dp + 9) % DP, cut(p)].astype(BF16)
            copy_l(0, p).start()

        def step_r(s, p):
            copy_r(s - 1, p).wait_recv()
            held = take_r[s - 1, cut(p)].astype(F32)
            give_r[s, cut(p)] = (held + local[(dp + 8 + DP - s) % DP, cut(p)]).astype(BF16)
            copy_r(s, p).start()

        def step_l(s, p):
            copy_l(s - 1, p).wait_recv()
            held = take_l[s - 1, cut(p)].astype(F32)
            give_l[s, cut(p)] = (held + local[(dp + 9 + s) % DP, cut(p)]).astype(BF16)
            copy_l(s, p).start()

        def step(s, _):
            for p in range(parts):
                step_r(s, p)
                step_l(s, p)
            return 0

        lax.fori_loop(1, Ring.LEFT, step, 0)
        for p in range(parts):
            step_r(Ring.LEFT, p)
        for p in range(parts):
            copy_l(Ring.LEFT - 1, p).wait_recv()
            copy_r(Ring.RIGHT - 1, p).wait_recv()
            both = take_l[Ring.LEFT - 1, cut(p)].astype(F32) + take_r[Ring.RIGHT - 1, cut(p)].astype(F32)
            put(cut(p), both + local[dp, cut(p)])

        def finish():
            def drain_r(s, _):
                for p in range(parts):
                    copy_r(s, p).wait_send()
                return 0

            def drain_l(s, _):
                for p in range(parts):
                    copy_l(s, p).wait_send()
                return 0

            lax.fori_loop(0, Ring.RIGHT, drain_r, 0)
            lax.fori_loop(0, Ring.LEFT, drain_l, 0)

        return finish

    def all_gather(whole, refs, rows, parts, between=()):
        sr, rr, sl, rl = refs
        dp, _, _, _ = place()
        right, left = {"dp": (dp + 1) % DP}, {"dp": (dp + DP - 1) % DP}
        piece = rows // parts

        def copy_r(s, p):
            part = whole.at[(dp + DP - s) % DP, pl.ds(p * piece, piece)]
            return send(part, part, sr.at[s, p], rr.at[s, p], right)

        def copy_l(s, p):
            part = whole.at[(dp + s) % DP, pl.ds(p * piece, piece)]
            return send(part, part, sl.at[s, p], rl.at[s, p], left)

        for p in range(parts):
            copy_r(0, p).start()
            copy_l(0, p).start()
        for s in range(1, Ring.RIGHT):
            for p in range(parts):
                copy_r(s - 1, p).wait_recv()
                copy_r(s, p).start()
                copy_l(s - 1, p).wait_recv()
                if s < Ring.LEFT:
                    copy_l(s, p).start()
            if s - 1 < len(between):
                between[s - 1]()
        for p in range(parts):
            copy_r(Ring.RIGHT - 1, p).wait_recv()

        def finish():
            def drain_r(s, _):
                for p in range(parts):
                    copy_r(s, p).wait_send()
                return 0

            def drain_l(s, _):
                for p in range(parts):
                    copy_l(s, p).wait_send()
                return 0

            lax.fori_loop(0, Ring.RIGHT, drain_r, 0)
            lax.fori_loop(0, Ring.LEFT, drain_l, 0)

        return finish


def half_rows(h):
    return pl.ds(pl.multiple_of(h * 256, 256), 256)


def dot_t(a, b):
    return lax.dot_general(a, b, (((0,), (0,)), ((), ())), preferred_element_type=F32)


N_PLANE = 9
N_SCATTER = 8
N_GATHER = 4


def sketch_kernel(og, tm, act, sketch, gram, *refs):
    plane_one = refs[:N_PLANE]
    plane_two = refs[N_PLANE : 2 * N_PLANE]
    rest = refs[2 * N_PLANE :]
    scatter, gather = rest[:N_SCATTER], rest[N_SCATTER : N_SCATTER + N_GATHER]
    sketch_in, local, gram_local = rest[N_SCATTER + N_GATHER :]
    dp, mp, chip, core = place()
    barrier, count = greet("ends")
    pl.semaphore_wait(barrier, count)

    def in_half(h):
        return jnp.dot(og[half_rows(h), :], tm[...], preferred_element_type=F32)

    def near_half():
        local[...] = dot_t(act[half_rows(core), :], sketch_in[half_rows(core), :]).reshape(DP, 16, R)

    done_one = PlaneSum.run(in_half, sketch_in, BF16, plane_one, near_half)
    far = half_rows(1 - core)
    local[...] += dot_t(act[far, :], sketch_in[far, :]).reshape(DP, 16, R)

    def put(rows, total):
        sketch[dp, rows] = total.astype(BF16)

    done_scatter = Ring.reduce_scatter(local, scatter, 16, 1, put)
    done_gather = Ring.all_gather(sketch, gather, 16, 1)
    rows_block = sketch[...].reshape(256, R)
    gram_local[...] = dot_t(rows_block, rows_block)

    def gram_half(h):
        return gram_local[half_rows(h), :]

    done_two = PlaneSum.run(gram_half, gram, F32, plane_two)
    done_one()
    done_scatter()
    done_gather()
    done_two()


VMEM = pl.BlockSpec(memory_space=pltpu.VMEM)


def sketch_call(out_grads, test_matrix, activations):
    return pl.pallas_call(
        sketch_kernel,
        out_shape=(
            jax.ShapeDtypeStruct((DP, 16, R), BF16),
            jax.ShapeDtypeStruct((R, R), F32),
        ),
        in_specs=[VMEM] * 3,
        out_specs=(VMEM, VMEM),
        scratch_shapes=[
            *PlaneSum.scratch(BF16),
            *PlaneSum.scratch(F32),
            *Ring.scratch_scatter(16, R, 1),
            *Ring.scratch_gather(1),
            pltpu.VMEM((R, R), BF16),
            pltpu.VMEM((DP, 16, R), F32),
            pltpu.VMEM((R, R), F32),
        ],
        compiler_params=pltpu.CompilerParams(
            collective_id=0, has_side_effects=True, vmem_limit_bytes=40 * 2**20
        ),
        name="sketch_and_gram",
    )(out_grads, test_matrix, activations)


def adam_kernel(act, basis, og, first, second, update, new_first, new_second, *refs):
    plane = refs[:N_PLANE]
    rest = refs[N_PLANE:]
    scatter, gather = rest[:N_SCATTER], rest[N_SCATTER : N_SCATTER + N_GATHER]
    rest = rest[N_SCATTER + N_GATHER :]
    coords, local, whole, slots, ss, sr, slot_pair, tiles, landed, sq_pair, qs, qr, zs, zr = rest
    dp, mp, chip, core = place()
    partner = {"mp": chip * 2 + 1 - core}
    barrier, count = greet("all")
    pl.semaphore_wait(barrier, count)

    def coords_half(h):
        return jnp.dot(act[half_rows(h), :], basis[...], preferred_element_type=F32)

    done_plane = PlaneSum.run(coords_half, coords, BF16, plane)

    slots[chip, core] = basis[pl.ds(pl.multiple_of(dp * 16, 16), 16), :]
    slot_gather = plane_gather(slots.at[chip, core], ss, sr)

    local[...] = dot_t(coords[...], og[...]).reshape(DP, 32, og.shape[1])
    squares = []

    def put(rows, projected):
        new_m = beta_one * first[rows, :] + (1.0 - beta_one) * projected
        new_v = beta_two * second[rows, :] + (1.0 - beta_two) * projected * projected
        new_first[rows, :] = new_m
        new_second[rows, :] = new_v
        correct_one = 1.0 - beta_one**STEP
        correct_two = 1.0 - beta_two**STEP
        direction = new_m / correct_one / (jnp.sqrt(new_v / correct_two) + adam_eps)
        squares.append(jnp.sum(direction * direction, keepdims=True))
        whole[dp, rows] = direction.astype(BF16)

    done_scatter = Ring.reduce_scatter(local, scatter, 32, 2, put)

    pair_copy = send(tiles.at[0], landed.at[0], sq_pair.at[0], sq_pair.at[1], partner)

    def chip_copy(k):
        return send(
            tiles.at[1], landed.at[k], qs.at[k - 1], qr.at[k - 1], {"mp": chip_at(chip, k) * 2 + core}
        )

    def plane_copy(k):
        return send(
            tiles.at[2], landed.at[15 + k], zs.at[k - 1], zr.at[k - 1], {"dp": (dp + k) % DP}
        )

    def start_all(copy):
        def go(k, _):
            copy(k).start()
            return 0

        lax.fori_loop(1, 16, go, 0)

    def add_all(copy, base, total):
        def go(k, value):
            copy(k).wait_recv()
            return value + landed[base + k]

        return lax.fori_loop(1, 16, go, total)

    slot_half = slots.at[:, core]
    slot_swap = send(slot_half, slot_half, slot_pair.at[0], slot_pair.at[1], partner)

    def after_one():
        pair_copy.wait_recv()
        tiles[1] = tiles[0] + landed[0]
        start_all(chip_copy)

    def after_two():
        wait_all(slot_gather, 1, CHIPS)
        slot_swap.start()

    def after_three():
        tiles[2] = add_all(chip_copy, 0, tiles[1])
        start_all(plane_copy)

    tiles[0] = jnp.broadcast_to(sum(squares), (8, 128))
    pair_copy.start()
    done_gather = Ring.all_gather(whole, gather, 32, 2, (after_one, after_two, after_three))
    slot_swap.wait_recv()
    total_squares = add_all(plane_copy, 15, tiles[2])
    factor = lax.rsqrt(total_squares / (R * FF) + norm_eps)[0:1, 0:1]
    rows_of = slots[...].reshape(R, R)
    product = jnp.dot(rows_of, whole[...].reshape(R, og.shape[1]), preferred_element_type=F32)
    update[...] = (factor * product).astype(BF16)

    done_plane()
    done_scatter()
    done_gather()
    wait_all(slot_gather, 1, CHIPS, recv=False)
    slot_swap.wait_send()
    pair_copy.wait_send()
    wait_all(chip_copy, 1, 16, recv=False)
    wait_all(plane_copy, 1, 16, recv=False)


def adam_call(activations, basis, out_grads, first, second):
    width = out_grads.shape[1]
    return pl.pallas_call(
        adam_kernel,
        out_shape=(
            jax.ShapeDtypeStruct((R, width), BF16),
            jax.ShapeDtypeStruct(first.shape, F32),
            jax.ShapeDtypeStruct(second.shape, F32),
        ),
        in_specs=[VMEM] * 5,
        out_specs=(VMEM,) * 3,
        scratch_shapes=[
            *PlaneSum.scratch(BF16),
            *Ring.scratch_scatter(32, width, 2),
            *Ring.scratch_gather(2),
            pltpu.VMEM((R, R), BF16),
            pltpu.VMEM((DP, 32, width), F32),
            pltpu.VMEM((DP, 32, width), BF16),
            pltpu.VMEM((CHIPS, 2, 16, R), BF16),
            pltpu.SemaphoreType.DMA((CHIPS - 1,)),
            pltpu.SemaphoreType.DMA((CHIPS - 1,)),
            pltpu.SemaphoreType.DMA((2,)),
            pltpu.VMEM((3, 8, 128), F32),
            pltpu.VMEM((31, 8, 128), F32),
            pltpu.SemaphoreType.DMA((2,)),
            pltpu.SemaphoreType.DMA((15,)),
            pltpu.SemaphoreType.DMA((15,)),
            pltpu.SemaphoreType.DMA((15,)),
            pltpu.SemaphoreType.DMA((15,)),
        ],
        compiler_params=pltpu.CompilerParams(
            collective_id=1, has_side_effects=True, vmem_limit_bytes=40 * 2**20
        ),
        name="project_and_update",
    )(activations, basis, out_grads, first, second)


def orthonormal(rows_block, gram_matrix):
    lower_factor = jnp.linalg.cholesky(gram_matrix)
    return lax.linalg.triangular_solve(
        lower_factor, rows_block, left_side=False, lower=True, transpose_a=True
    )


def shards(activations, out_grads, test_matrix, first_moment, second_moment):
    sketch, gram_matrix = sketch_call(out_grads, test_matrix, activations)
    rows_block = sketch.reshape(activations.shape[1], R).astype(F32)
    basis_b = orthonormal(rows_block, gram_matrix).astype(BF16)
    update, new_first, new_second = adam_call(
        activations, basis_b, out_grads, first_moment, second_moment
    )
    return (update.reshape(lax.axis_size("mp"), 16, out_grads.shape[1]), new_first, new_second)


def solution(mesh):
    placed = (P("dp", "mp"), P("dp", "mp"), P("mp", None), P("dp", "mp"), P("dp", "mp"))
    return jax.shard_map(
        shards,
        mesh=mesh,
        in_specs=placed,
        out_specs=(P(None, "dp", "mp"), P("dp", "mp"), P("dp", "mp")),
        check_vma=False,
    )
```

```python
import jax
import jax.numpy as jnp
from jax import lax
from jax.experimental import pallas as pl
from jax.experimental.pallas import tpu as pltpu
from jax.sharding import PartitionSpec as P

FF = 29568
R = 512
STEP = 100

beta_one = 0.9
beta_two = 0.999
adam_eps = 1e-08
norm_eps = 1e-06

MESH = pl.DeviceIdType.MESH
F32 = jnp.float32
BF16 = jnp.bfloat16
CHIPS = 16
DP = 16


def place():
    mp = lax.axis_index("mp")
    core = mp % 2
    chip = mp // 2
    return lax.axis_index("dp"), mp, chip, core


def chip_at(chip, k):
    x = (chip // 4 + k // 4) % 4
    y = (chip % 4 + k % 4) % 4
    return x * 4 + y


def greet(dp_offsets):
    dp, mp, chip, core = place()
    barrier = pltpu.get_barrier_semaphore()
    pl.semaphore_signal(barrier, inc=1, device_id={"mp": chip * 2 + 1 - core}, device_id_type=MESH)

    def to_chip(k, _):
        pl.semaphore_signal(
            barrier, inc=1, device_id={"mp": chip_at(chip, k) * 2 + core}, device_id_type=MESH
        )
        return 0

    lax.fori_loop(1, CHIPS, to_chip, 0)

    def to_ring(k, _):
        pl.semaphore_signal(barrier, inc=1, device_id={"dp": (dp + k) % DP}, device_id_type=MESH)
        return 0

    if dp_offsets == "all":
        lax.fori_loop(1, DP, to_ring, 0)
        return barrier, 1 + (CHIPS - 1) + (DP - 1)
    to_ring(1, 0)
    to_ring(DP - 1, 0)
    return barrier, 1 + (CHIPS - 1) + 2


def send(src, dst, sends, recvs, where):
    return pltpu.make_async_remote_copy(
        src_ref=src, dst_ref=dst, send_sem=sends, recv_sem=recvs, device_id=where, device_id_type=MESH
    )


def plane_scatter(stage, landed, sends, recvs):
    _, _, chip, core = place()

    def copy(k):
        there = chip_at(chip, k)
        return send(
            stage.at[there], landed.at[k - 1], sends.at[k - 1], recvs.at[k - 1], {"mp": there * 2 + core}
        )

    def go(k, _):
        copy(k).start()
        return 0

    lax.fori_loop(1, CHIPS, go, 0)
    return copy


def plane_gather(block, sends, recvs):
    _, _, chip, core = place()

    def copy(k):
        there = chip_at(chip, k)
        return send(block, block, sends.at[k - 1], recvs.at[k - 1], {"mp": there * 2 + core})

    def go(k, _):
        copy(k).start()
        return 0

    lax.fori_loop(1, CHIPS, go, 0)
    return copy


def wait_all(copy, first, last, recv=True):
    def step(k, _):
        if recv:
            copy(k).wait_recv()
        else:
            copy(k).wait_send()
        return 0

    lax.fori_loop(first, last, step, 0)


class PlaneSum:
    def scratch(kind):
        return [
            pltpu.VMEM((256, R), kind),
            pltpu.VMEM((256, R), kind),
            pltpu.VMEM((CHIPS, 16, R), kind),
            pltpu.VMEM((CHIPS - 1, 16, R), kind),
            pltpu.SemaphoreType.DMA((4,)),
            pltpu.SemaphoreType.DMA((CHIPS - 1,)),
            pltpu.SemaphoreType.DMA((CHIPS - 1,)),
            pltpu.SemaphoreType.DMA((CHIPS - 1,)),
            pltpu.SemaphoreType.DMA((CHIPS - 1,)),
        ]

    def run(half_of, full, kind, refs, between=None):
        give, take, stage, landed, pair_sems, s1, r1, s2, r2 = refs
        dp, mp, chip, core = place()
        partner = {"mp": chip * 2 + 1 - core}
        give[...] = half_of(1 - core).astype(kind)
        swap = send(give, take, pair_sems.at[0], pair_sems.at[1], partner)
        swap.start()
        own = half_of(core)
        swap.wait_recv()
        stage[...] = (own + take[...].astype(F32)).astype(kind).reshape(CHIPS, 16, R)
        scatter = plane_scatter(stage, landed, s1, r1)

        def add(k, total):
            scatter(k).wait_recv()
            return total + landed[k - 1].astype(F32)

        total = lax.fori_loop(1, CHIPS, add, stage[chip].astype(F32))
        mine = pl.ds(pl.multiple_of(core * 256 + chip * 16, 16), 16)
        full[mine, :] = total.astype(kind)
        gather = plane_gather(full.at[mine, :], s2, r2)
        wait_all(gather, 1, CHIPS)
        half = full.at[pl.ds(pl.multiple_of(core * 256, 256), 256), :]
        swap_full = send(half, half, pair_sems.at[2], pair_sems.at[3], partner)
        swap_full.start()
        if between is not None:
            between()
        swap_full.wait_recv()

        def finish():
            swap.wait_send()
            wait_all(scatter, 1, CHIPS, recv=False)
            wait_all(gather, 1, CHIPS, recv=False)
            swap_full.wait_send()

        return finish


class Ring:
    RIGHT, LEFT = 8, 7

    def scratch_scatter(rows, width, parts):
        return [
            pltpu.VMEM((Ring.RIGHT, rows, width), BF16),
            pltpu.VMEM((Ring.RIGHT, rows, width), BF16),
            pltpu.VMEM((Ring.LEFT, rows, width), BF16),
            pltpu.VMEM((Ring.LEFT, rows, width), BF16),
            pltpu.SemaphoreType.DMA((Ring.RIGHT, parts)),
            pltpu.SemaphoreType.DMA((Ring.RIGHT, parts)),
            pltpu.SemaphoreType.DMA((Ring.LEFT, parts)),
            pltpu.SemaphoreType.DMA((Ring.LEFT, parts)),
        ]

    def scratch_gather(parts):
        return [
            pltpu.SemaphoreType.DMA((Ring.RIGHT, parts)),
            pltpu.SemaphoreType.DMA((Ring.RIGHT, parts)),
            pltpu.SemaphoreType.DMA((Ring.LEFT, parts)),
            pltpu.SemaphoreType.DMA((Ring.LEFT, parts)),
        ]

    def reduce_scatter(local, refs, rows, parts, put):
        give_r, take_r, give_l, take_l, sr, rr, sl, rl = refs
        dp, _, _, _ = place()
        right, left = {"dp": (dp + 1) % DP}, {"dp": (dp + DP - 1) % DP}
        piece = rows // parts

        def cut(p):
            return pl.ds(p * piece, piece)

        def copy_r(s, p):
            return send(
                give_r.at[s, cut(p)], take_r.at[s, cut(p)], sr.at[s, p], rr.at[s, p], right
            )

        def copy_l(s, p):
            return send(
                give_l.at[s, cut(p)], take_l.at[s, cut(p)], sl.at[s, p], rl.at[s, p], left
            )

        for p in range(parts):
            give_r[0, cut(p)] = local[(dp + 8) % DP, cut(p)].astype(BF16)
            copy_r(0, p).start()
            give_l[0, cut(p)] = local[(dp + 9) % DP, cut(p)].astype(BF16)
            copy_l(0, p).start()

        def step_r(s, p):
            copy_r(s - 1, p).wait_recv()
            held = take_r[s - 1, cut(p)].astype(F32)
            give_r[s, cut(p)] = (held + local[(dp + 8 + DP - s) % DP, cut(p)]).astype(BF16)
            copy_r(s, p).start()

        def step_l(s, p):
            copy_l(s - 1, p).wait_recv()
            held = take_l[s - 1, cut(p)].astype(F32)
            give_l[s, cut(p)] = (held + local[(dp + 9 + s) % DP, cut(p)]).astype(BF16)
            copy_l(s, p).start()

        def step(s, _):
            for p in range(parts):
                step_r(s, p)
                step_l(s, p)
            return 0

        lax.fori_loop(1, Ring.LEFT, step, 0)
        for p in range(parts):
            step_r(Ring.LEFT, p)
        for p in range(parts):
            copy_l(Ring.LEFT - 1, p).wait_recv()
            copy_r(Ring.RIGHT - 1, p).wait_recv()
            both = take_l[Ring.LEFT - 1, cut(p)].astype(F32) + take_r[Ring.RIGHT - 1, cut(p)].astype(F32)
            put(cut(p), both + local[dp, cut(p)])

        def finish():
            def drain_r(s, _):
                for p in range(parts):
                    copy_r(s, p).wait_send()
                return 0

            def drain_l(s, _):
                for p in range(parts):
                    copy_l(s, p).wait_send()
                return 0

            lax.fori_loop(0, Ring.RIGHT, drain_r, 0)
            lax.fori_loop(0, Ring.LEFT, drain_l, 0)

        return finish

    def all_gather(whole, refs, rows, parts, between=()):
        sr, rr, sl, rl = refs
        dp, _, _, _ = place()
        right, left = {"dp": (dp + 1) % DP}, {"dp": (dp + DP - 1) % DP}
        piece = rows // parts

        def copy_r(s, p):
            part = whole.at[(dp + DP - s) % DP, pl.ds(p * piece, piece)]
            return send(part, part, sr.at[s, p], rr.at[s, p], right)

        def copy_l(s, p):
            part = whole.at[(dp + s) % DP, pl.ds(p * piece, piece)]
            return send(part, part, sl.at[s, p], rl.at[s, p], left)

        for p in range(parts):
            copy_r(0, p).start()
            copy_l(0, p).start()
        for s in range(1, Ring.RIGHT):
            for p in range(parts):
                copy_r(s - 1, p).wait_recv()
                copy_r(s, p).start()
                copy_l(s - 1, p).wait_recv()
                if s < Ring.LEFT:
                    copy_l(s, p).start()
            if s - 1 < len(between):
                between[s - 1]()
        for p in range(parts):
            copy_r(Ring.RIGHT - 1, p).wait_recv()

        def finish():
            def drain_r(s, _):
                for p in range(parts):
                    copy_r(s, p).wait_send()
                return 0

            def drain_l(s, _):
                for p in range(parts):
                    copy_l(s, p).wait_send()
                return 0

            lax.fori_loop(0, Ring.RIGHT, drain_r, 0)
            lax.fori_loop(0, Ring.LEFT, drain_l, 0)

        return finish


def half_rows(h):
    return pl.ds(pl.multiple_of(h * 256, 256), 256)


def dot_t(a, b):
    return lax.dot_general(a, b, (((0,), (0,)), ((), ())), preferred_element_type=F32)


N_PLANE = 9
N_SCATTER = 8
N_GATHER = 4


def sketch_kernel(og, tm, act, sketch, gram, *refs):
    plane_one = refs[:N_PLANE]
    plane_two = refs[N_PLANE : 2 * N_PLANE]
    rest = refs[2 * N_PLANE :]
    scatter, gather = rest[:N_SCATTER], rest[N_SCATTER : N_SCATTER + N_GATHER]
    sketch_in, local, gram_local = rest[N_SCATTER + N_GATHER :]
    dp, mp, chip, core = place()
    barrier, count = greet("ends")
    pl.semaphore_wait(barrier, count)

    def in_half(h):
        return jnp.dot(og[half_rows(h), :], tm[...], preferred_element_type=F32)

    def near_half():
        local[...] = dot_t(act[half_rows(core), :], sketch_in[half_rows(core), :]).reshape(DP, 16, R)

    done_one = PlaneSum.run(in_half, sketch_in, BF16, plane_one, near_half)
    far = half_rows(1 - core)
    local[...] += dot_t(act[far, :], sketch_in[far, :]).reshape(DP, 16, R)

    def put(rows, total):
        sketch[dp, rows] = total.astype(BF16)

    done_scatter = Ring.reduce_scatter(local, scatter, 16, 1, put)
    done_gather = Ring.all_gather(sketch, gather, 16, 1)
    rows_block = sketch[...].reshape(256, R)
    gram_local[...] = dot_t(rows_block, rows_block)

    def gram_half(h):
        return gram_local[half_rows(h), :]

    done_two = PlaneSum.run(gram_half, gram, F32, plane_two)
    done_one()
    done_scatter()
    done_gather()
    done_two()


VMEM = pl.BlockSpec(memory_space=pltpu.VMEM)


def sketch_call(out_grads, test_matrix, activations):
    return pl.pallas_call(
        sketch_kernel,
        out_shape=(
            jax.ShapeDtypeStruct((DP, 16, R), BF16),
            jax.ShapeDtypeStruct((R, R), F32),
        ),
        in_specs=[VMEM] * 3,
        out_specs=(VMEM, VMEM),
        scratch_shapes=[
            *PlaneSum.scratch(BF16),
            *PlaneSum.scratch(F32),
            *Ring.scratch_scatter(16, R, 1),
            *Ring.scratch_gather(1),
            pltpu.VMEM((R, R), BF16),
            pltpu.VMEM((DP, 16, R), F32),
            pltpu.VMEM((R, R), F32),
        ],
        compiler_params=pltpu.CompilerParams(
            collective_id=0, has_side_effects=True, vmem_limit_bytes=40 * 2**20
        ),
        name="sketch_and_gram",
    )(out_grads, test_matrix, activations)


def adam_kernel(act, basis, og, first, second, update, new_first, new_second, *refs):
    plane = refs[:N_PLANE]
    rest = refs[N_PLANE:]
    scatter, gather = rest[:N_SCATTER], rest[N_SCATTER : N_SCATTER + N_GATHER]
    rest = rest[N_SCATTER + N_GATHER :]
    coords, local, whole, slots, ss, sr, slot_pair, tiles, landed, sq_pair, qs, qr, zs, zr = rest
    dp, mp, chip, core = place()
    partner = {"mp": chip * 2 + 1 - core}
    barrier, count = greet("all")
    pl.semaphore_wait(barrier, count)

    def coords_half(h):
        return jnp.dot(act[half_rows(h), :], basis[...], preferred_element_type=F32)

    done_plane = PlaneSum.run(coords_half, coords, BF16, plane)

    slots[chip, core] = basis[pl.ds(pl.multiple_of(dp * 16, 16), 16), :]
    slot_gather = plane_gather(slots.at[chip, core], ss, sr)

    local[...] = dot_t(coords[...], og[...]).reshape(DP, 32, og.shape[1])
    squares = []

    def put(rows, projected):
        new_m = beta_one * first[rows, :] + (1.0 - beta_one) * projected
        new_v = beta_two * second[rows, :] + (1.0 - beta_two) * projected * projected
        new_first[rows, :] = new_m
        new_second[rows, :] = new_v
        correct_one = 1.0 - beta_one**STEP
        correct_two = 1.0 - beta_two**STEP
        direction = new_m / correct_one / (jnp.sqrt(new_v / correct_two) + adam_eps)
        squares.append(jnp.sum(direction * direction, keepdims=True))
        whole[dp, rows] = direction.astype(BF16)

    done_scatter = Ring.reduce_scatter(local, scatter, 32, 2, put)

    pair_copy = send(tiles.at[0], landed.at[0], sq_pair.at[0], sq_pair.at[1], partner)

    def chip_copy(k):
        return send(
            tiles.at[1], landed.at[k], qs.at[k - 1], qr.at[k - 1], {"mp": chip_at(chip, k) * 2 + core}
        )

    def plane_copy(k):
        return send(
            tiles.at[2], landed.at[15 + k], zs.at[k - 1], zr.at[k - 1], {"dp": (dp + k) % DP}
        )

    def start_all(copy):
        def go(k, _):
            copy(k).start()
            return 0

        lax.fori_loop(1, 16, go, 0)

    def add_all(copy, base, total):
        def go(k, value):
            copy(k).wait_recv()
            return value + landed[base + k]

        return lax.fori_loop(1, 16, go, total)

    slot_half = slots.at[:, core]
    slot_swap = send(slot_half, slot_half, slot_pair.at[0], slot_pair.at[1], partner)

    def after_one():
        pair_copy.wait_recv()
        tiles[1] = tiles[0] + landed[0]
        start_all(chip_copy)

    def after_two():
        wait_all(slot_gather, 1, CHIPS)
        slot_swap.start()

    def after_three():
        tiles[2] = add_all(chip_copy, 0, tiles[1])
        start_all(plane_copy)

    tiles[0] = jnp.broadcast_to(sum(squares), (8, 128))
    pair_copy.start()
    done_gather = Ring.all_gather(whole, gather, 32, 2, (after_one, after_two, after_three))
    slot_swap.wait_recv()
    total_squares = add_all(plane_copy, 15, tiles[2])
    factor = lax.rsqrt(total_squares / (R * FF) + norm_eps)[0:1, 0:1]
    rows_of = slots[...].reshape(R, R)
    product = jnp.dot(rows_of, whole[...].reshape(R, og.shape[1]), preferred_element_type=F32)
    update[...] = (factor * product).astype(BF16)

    done_plane()
    done_scatter()
    done_gather()
    wait_all(slot_gather, 1, CHIPS, recv=False)
    slot_swap.wait_send()
    pair_copy.wait_send()
    wait_all(chip_copy, 1, 16, recv=False)
    wait_all(plane_copy, 1, 16, recv=False)


def adam_call(activations, basis, out_grads, first, second):
    width = out_grads.shape[1]
    return pl.pallas_call(
        adam_kernel,
        out_shape=(
            jax.ShapeDtypeStruct((R, width), BF16),
            jax.ShapeDtypeStruct(first.shape, F32),
            jax.ShapeDtypeStruct(second.shape, F32),
        ),
        in_specs=[VMEM] * 5,
        out_specs=(VMEM,) * 3,
        scratch_shapes=[
            *PlaneSum.scratch(BF16),
            *Ring.scratch_scatter(32, width, 2),
            *Ring.scratch_gather(2),
            pltpu.VMEM((R, R), BF16),
            pltpu.VMEM((DP, 32, width), F32),
            pltpu.VMEM((DP, 32, width), BF16),
            pltpu.VMEM((CHIPS, 2, 16, R), BF16),
            pltpu.SemaphoreType.DMA((CHIPS - 1,)),
            pltpu.SemaphoreType.DMA((CHIPS - 1,)),
            pltpu.SemaphoreType.DMA((2,)),
            pltpu.VMEM((3, 8, 128), F32),
            pltpu.VMEM((31, 8, 128), F32),
            pltpu.SemaphoreType.DMA((2,)),
            pltpu.SemaphoreType.DMA((15,)),
            pltpu.SemaphoreType.DMA((15,)),
            pltpu.SemaphoreType.DMA((15,)),
            pltpu.SemaphoreType.DMA((15,)),
        ],
        compiler_params=pltpu.CompilerParams(
            collective_id=1, has_side_effects=True, vmem_limit_bytes=40 * 2**20
        ),
        name="project_and_update",
    )(activations, basis, out_grads, first, second)


LEAF = 128


def exact_dot(a, b, dims):
    return lax.dot_general(
        a, b, (dims, ((), ())), precision=lax.Precision.HIGHEST, preferred_element_type=F32
    )


def leaf_inverse(block, inverse):
    groups = LEAF // 8
    sub = lax.broadcasted_iota(jnp.int32, (8, 128), 0)

    def spread(row):
        return jnp.broadcast_to(row, (8, 128))

    for p in range(groups):
        cols = {
            g: [spread(block[g][:, 8 * p + j : 8 * p + j + 1]) for j in range(8)]
            for g in range(p, groups)
        }
        pivots = jnp.zeros((8, 128), F32)
        for j in range(8):
            pivot = spread(cols[p][j][j : j + 1, :])
            over = 1.0 / pivot
            pivots = jnp.where(sub == j, pivot, pivots)
            below = jnp.where(sub > j, cols[p][j], 0.0)
            row_block = spread(block[p][j : j + 1, :]) * over
            row_inverse = spread(inverse[p][j : j + 1, :]) * over
            ratio = {i: spread(cols[p][j][i : i + 1, :]) * over for i in range(j + 1, 8)}
            for g in range(p, groups):
                left = below if g == p else cols[g][j]
                for i in range(j + 1, 8):
                    cols[g][i] = cols[g][i] - left * ratio[i]
                block[g] = block[g] - left * row_block
                inverse[g] = inverse[g] - left * row_inverse
        inverse[p] = inverse[p] * lax.rsqrt(pivots)
    return jnp.concatenate(inverse, axis=0)


def basis_kernel(gram, sketch, basis, whole):
    whole[:, :R] = gram[...]
    whole[:, R:] = sketch[...].astype(F32).T
    lane = lax.broadcasted_iota(jnp.int32, (8, 128), 1)
    sub = lax.broadcasted_iota(jnp.int32, (8, 128), 0)
    for k in range(R // LEAF):
        here, after = k * LEAF, (k + 1) * LEAF
        block = [whole[here + 8 * g : here + 8 * g + 8, here:after] for g in range(LEAF // 8)]
        unit = [jnp.where(lane == sub + 8 * g, 1.0, 0.0) for g in range(LEAF // 8)]
        inverse = leaf_inverse(block, unit)
        panel = exact_dot(inverse, whole[here:after, after:], ((1,), (0,)))
        tail = R - after
        if tail:
            whole[after:, after:] -= exact_dot(panel[:, :tail], panel, ((0,), (0,)))
        basis[:, here:after] = panel[:, tail:].T.astype(BF16)


def basis_call(gram_matrix, sketch):
    return pl.pallas_call(
        basis_kernel,
        out_shape=jax.ShapeDtypeStruct(sketch.shape, BF16),
        in_specs=[VMEM] * 2,
        out_specs=VMEM,
        scratch_shapes=[pltpu.VMEM((R, R + sketch.shape[0]), F32)],
        compiler_params=pltpu.CompilerParams(vmem_limit_bytes=40 * 2**20),
        name="orthonormal",
    )(gram_matrix, sketch)


def shards(activations, out_grads, test_matrix, first_moment, second_moment):
    sketch, gram_matrix = sketch_call(out_grads, test_matrix, activations)
    basis_b = basis_call(gram_matrix, sketch.reshape(activations.shape[1], R))
    update, new_first, new_second = adam_call(
        activations, basis_b, out_grads, first_moment, second_moment
    )
    return (update.reshape(lax.axis_size("mp"), 16, out_grads.shape[1]), new_first, new_second)


def solution(mesh):
    placed = (P("dp", "mp"), P("dp", "mp"), P("mp", None), P("dp", "mp"), P("dp", "mp"))
    return jax.shard_map(
        shards,
        mesh=mesh,
        in_specs=placed,
        out_specs=(P(None, "dp", "mp"), P("dp", "mp"), P("dp", "mp")),
        check_vma=False,
    )
```

```python
import jax
import jax.numpy as jnp
from jax import lax
from jax.experimental import pallas as pl
from jax.experimental.pallas import tpu as pltpu
from jax.sharding import PartitionSpec as P

FF = 29568
R = 512
STEP = 100

beta_one = 0.9
beta_two = 0.999
adam_eps = 1e-08
norm_eps = 1e-06

MESH = pl.DeviceIdType.MESH
F32 = jnp.float32
BF16 = jnp.bfloat16
CHIPS = 16
DP = 16


def place():
    mp = lax.axis_index("mp")
    core = mp % 2
    chip = mp // 2
    return lax.axis_index("dp"), mp, chip, core


def chip_at(chip, k):
    x = (chip // 4 + k // 4) % 4
    y = (chip % 4 + k % 4) % 4
    return x * 4 + y


def greet(dp_offsets):
    dp, mp, chip, core = place()
    barrier = pltpu.get_barrier_semaphore()
    pl.semaphore_signal(barrier, inc=1, device_id={"mp": chip * 2 + 1 - core}, device_id_type=MESH)

    def to_chip(k, _):
        pl.semaphore_signal(
            barrier, inc=1, device_id={"mp": chip_at(chip, k) * 2 + core}, device_id_type=MESH
        )
        return 0

    lax.fori_loop(1, CHIPS, to_chip, 0)

    def to_ring(k, _):
        pl.semaphore_signal(barrier, inc=1, device_id={"dp": (dp + k) % DP}, device_id_type=MESH)
        return 0

    if dp_offsets == "all":
        lax.fori_loop(1, DP, to_ring, 0)
        return barrier, 1 + (CHIPS - 1) + (DP - 1)
    to_ring(1, 0)
    to_ring(DP - 1, 0)
    return barrier, 1 + (CHIPS - 1) + 2


def send(src, dst, sends, recvs, where):
    return pltpu.make_async_remote_copy(
        src_ref=src, dst_ref=dst, send_sem=sends, recv_sem=recvs, device_id=where, device_id_type=MESH
    )


def plane_scatter(stage, landed, sends, recvs):
    _, _, chip, core = place()

    def copy(k):
        there = chip_at(chip, k)
        return send(
            stage.at[there], landed.at[k - 1], sends.at[k - 1], recvs.at[k - 1], {"mp": there * 2 + core}
        )

    def go(k, _):
        copy(k).start()
        return 0

    lax.fori_loop(1, CHIPS, go, 0)
    return copy


def plane_gather(block, sends, recvs):
    _, _, chip, core = place()

    def copy(k):
        there = chip_at(chip, k)
        return send(block, block, sends.at[k - 1], recvs.at[k - 1], {"mp": there * 2 + core})

    def go(k, _):
        copy(k).start()
        return 0

    lax.fori_loop(1, CHIPS, go, 0)
    return copy


def wait_all(copy, first, last, recv=True):
    def step(k, _):
        if recv:
            copy(k).wait_recv()
        else:
            copy(k).wait_send()
        return 0

    lax.fori_loop(first, last, step, 0)


class PlaneSum:
    COUNT = 9

    def scratch(kind):
        return [
            pltpu.VMEM((256, R), kind),
            pltpu.VMEM((256, R), kind),
            pltpu.VMEM((CHIPS, 16, R), kind),
            pltpu.VMEM((CHIPS - 1, 16, R), kind),
            pltpu.SemaphoreType.DMA((4,)),
            pltpu.SemaphoreType.DMA((CHIPS - 1,)),
            pltpu.SemaphoreType.DMA((CHIPS - 1,)),
            pltpu.SemaphoreType.DMA((CHIPS - 1,)),
            pltpu.SemaphoreType.DMA((CHIPS - 1,)),
        ]

    def __init__(self, half_of, full, kind, refs):
        self.half_of, self.full, self.kind = half_of, full, kind
        self.give, self.take, self.stage, self.landed, pair, self.s1, self.r1, self.s2, self.r2 = refs
        _, _, self.chip, self.core = place()
        partner = {"mp": self.chip * 2 + 1 - self.core}
        self.swap = send(self.give, self.take, pair.at[0], pair.at[1], partner)
        half = full.at[half_rows(self.core), :]
        self.swap_full = send(half, half, pair.at[2], pair.at[3], partner)

    def start(self):
        self.give[...] = self.half_of(1 - self.core).astype(self.kind)
        self.swap.start()

    def scatter(self):
        own = self.half_of(self.core)
        self.swap.wait_recv()
        both = own + self.take[...].astype(F32)
        self.stage[...] = both.astype(self.kind).reshape(CHIPS, 16, R)
        self.out = plane_scatter(self.stage, self.landed, self.s1, self.r1)

    def gather(self):
        def add(k, total):
            self.out(k).wait_recv()
            return total + self.landed[k - 1].astype(F32)

        total = lax.fori_loop(1, CHIPS, add, self.stage[self.chip].astype(F32))
        mine = pl.ds(pl.multiple_of(self.core * 256 + self.chip * 16, 16), 16)
        self.full[mine, :] = total.astype(self.kind)
        self.back = plane_gather(self.full.at[mine, :], self.s2, self.r2)

    def share(self):
        wait_all(self.back, 1, CHIPS)
        self.swap_full.start()

    def end(self):
        self.swap_full.wait_recv()

    def drain(self):
        self.swap.wait_send()
        wait_all(self.out, 1, CHIPS, recv=False)
        wait_all(self.back, 1, CHIPS, recv=False)
        self.swap_full.wait_send()


def to_ring(copy_to):
    def go(i, _):
        copy_to(8 + (2 * (i % 2) - 1) * ((i + 1) // 2)).start()
        return 0

    lax.fori_loop(0, DP - 1, go, 0)


class Ring:
    RIGHT, LEFT = 8, 7

    def scratch_gather(parts):
        return [
            pltpu.SemaphoreType.DMA((Ring.RIGHT, parts)),
            pltpu.SemaphoreType.DMA((Ring.RIGHT, parts)),
            pltpu.SemaphoreType.DMA((Ring.LEFT, parts)),
            pltpu.SemaphoreType.DMA((Ring.LEFT, parts)),
        ]

    def all_gather(whole, refs, rows, parts, between=()):
        sr, rr, sl, rl = refs
        dp, _, _, _ = place()
        right, left = {"dp": (dp + 1) % DP}, {"dp": (dp + DP - 1) % DP}
        piece = rows // parts

        def copy_r(s, p):
            part = whole.at[(dp + DP - s) % DP, pl.ds(p * piece, piece)]
            return send(part, part, sr.at[s, p], rr.at[s, p], right)

        def copy_l(s, p):
            part = whole.at[(dp + s) % DP, pl.ds(p * piece, piece)]
            return send(part, part, sl.at[s, p], rl.at[s, p], left)

        for p in range(parts):
            copy_r(0, p).start()
            copy_l(0, p).start()
        if between:
            between[0]()
        for s in range(1, Ring.RIGHT):
            for p in range(parts):
                copy_r(s - 1, p).wait_recv()
                copy_r(s, p).start()
                copy_l(s - 1, p).wait_recv()
                if s < Ring.LEFT:
                    copy_l(s, p).start()
            if s < len(between) and between[s] is not None:
                between[s]()
        for p in range(parts):
            copy_r(Ring.RIGHT - 1, p).wait_recv()

        def finish():
            def drain_r(s, _):
                for p in range(parts):
                    copy_r(s, p).wait_send()
                return 0

            def drain_l(s, _):
                for p in range(parts):
                    copy_l(s, p).wait_send()
                return 0

            lax.fori_loop(0, Ring.RIGHT, drain_r, 0)
            lax.fori_loop(0, Ring.LEFT, drain_l, 0)

        return finish


class FoldedScatter:
    COUNT = 9

    def scratch(rows, width):
        return [
            pltpu.VMEM((4, 3, rows, width), BF16),
            pltpu.VMEM((4, rows, width), BF16),
            pltpu.VMEM((3, rows, width), BF16),
            pltpu.VMEM((rows, width), F32),
            pltpu.SemaphoreType.DMA((4, 3)),
            pltpu.SemaphoreType.DMA((4, 3)),
            pltpu.SemaphoreType.DMA((3,)),
            pltpu.SemaphoreType.DMA((3,)),
            pltpu.VMEM((DP, rows, width), BF16),
        ]

    def __init__(self, local, refs):
        self.local = local
        self.near, self.stage, self.far, self.own, self.ns, self.nr, self.fs, self.fr, self.give = refs
        self.dp = lax.axis_index("dp")
        self.cls, self.row = self.dp % 4, self.dp // 4

    def near_copy(self, o, j):
        q = (self.row + o) % 4
        step = (1, DP - 1, DP - 2 + 4 * (q % 2))[j]
        to = (self.dp + step) % DP
        return send(
            self.give.at[to % 4 + 4 * q], self.near.at[q, j], self.ns.at[q, j], self.nr.at[q, j], {"dp": to}
        )

    def far_copy(self, o):
        q = (self.row + o) % 4
        return send(
            self.stage.at[q], self.far.at[o - 1], self.fs.at[o - 1], self.fr.at[o - 1],
            {"dp": self.cls + 4 * q},
        )

    def start(self):
        self.give[...] = self.local[...].astype(BF16)
        for o in (2, 1, 3, 0):
            for j in range(3):
                self.near_copy(o, j).start()

    def fold(self):
        for o in (2, 1, 3, 0):
            q = (self.row + o) % 4
            total = self.local[self.cls + 4 * q]
            for j in range(3):
                self.near_copy(o, j).wait_recv()
                total = total + self.near[q, j].astype(F32)
            if o:
                self.stage[q] = total.astype(BF16)
                self.far_copy(o).start()
            else:
                self.own[...] = total

    def end(self):
        total = self.own[...]
        for o in (1, 3, 2):
            self.far_copy(o).wait_recv()
            total = total + self.far[o - 1].astype(F32)
        return total

    def drain(self):
        for o in range(4):
            for j in range(3):
                self.near_copy(o, j).wait_send()
            if o:
                self.far_copy(o).wait_send()


def half_rows(h):
    return pl.ds(pl.multiple_of(h * 256, 256), 256)


def dot_t(a, b):
    return lax.dot_general(a, b, (((0,), (0,)), ((), ())), preferred_element_type=F32)


LEAF = 128


def exact_dot(a, b, dims):
    return lax.dot_general(
        a, b, (dims, ((), ())), precision=lax.Precision.HIGHEST, preferred_element_type=F32
    )


def leaf_inverse(block, inverse):
    groups = LEAF // 8
    sub = lax.broadcasted_iota(jnp.int32, (8, 128), 0)

    def spread(row):
        return jnp.broadcast_to(row, (8, 128))

    for p in range(groups):
        cols = {
            g: [spread(block[g][:, 8 * p + j : 8 * p + j + 1]) for j in range(8)]
            for g in range(p, groups)
        }
        pivots = jnp.zeros((8, 128), F32)
        for j in range(8):
            pivot = spread(cols[p][j][j : j + 1, :])
            over = 1.0 / pivot
            pivots = jnp.where(sub == j, pivot, pivots)
            below = jnp.where(sub > j, cols[p][j], 0.0)
            row_block = spread(block[p][j : j + 1, :]) * over
            row_inverse = spread(inverse[p][j : j + 1, :]) * over
            ratio = {i: spread(cols[p][j][i : i + 1, :]) * over for i in range(j + 1, 8)}
            for g in range(p, groups):
                left = below if g == p else cols[g][j]
                for i in range(j + 1, 8):
                    cols[g][i] = cols[g][i] - left * ratio[i]
                block[g] = block[g] - left * row_block
                inverse[g] = inverse[g] - left * row_inverse
        inverse[p] = inverse[p] * lax.rsqrt(pivots)
    return jnp.concatenate(inverse, axis=0)


VMEM = pl.BlockSpec(memory_space=pltpu.VMEM)


N_PLANE = PlaneSum.COUNT
N_FOLD = FoldedScatter.COUNT
N_GATHER = 4
SLICE = 64
WIDE = DP * SLICE


def dp_semaphores():
    return [pltpu.SemaphoreType.DMA((DP - 1,)) for _ in range(2)]


def invert_factor(whole, after_first):
    lane = lax.broadcasted_iota(jnp.int32, (8, 128), 1)
    sub = lax.broadcasted_iota(jnp.int32, (8, 128), 0)
    column = lax.broadcasted_iota(jnp.int32, (LEAF, R), 1)

    def step(k, _):
        here = pl.ds(pl.multiple_of(k * LEAF, LEAF), LEAF)
        corner = whole[here, here]
        block = [corner[8 * g : 8 * g + 8] for g in range(LEAF // 8)]
        unit = [jnp.where(lane == sub + 8 * g, 1.0, 0.0) for g in range(LEAF // 8)]
        inverse = leaf_inverse(block, unit)
        panel = exact_dot(inverse, whole[here, :], ((1,), (0,)))
        below = jnp.where(column >= (k + 1) * LEAF, panel[:, :R], 0.0)
        whole[here, R:] = panel[:, R:]
        whole[...] -= exact_dot(below, panel, ((0,), (0,)))

        @pl.when(k == 0)
        def _():
            after_first()

        return 0

    lax.fori_loop(0, R // LEAF, step, 0)


def galore_kernel(og, tm, act, first, second, update, new_first, new_second, *refs):
    sums = [refs[i * N_PLANE : (i + 1) * N_PLANE] for i in range(3)]
    rest = refs[3 * N_PLANE :]
    fold_refs, rest = rest[:N_FOLD], rest[N_FOLD:]
    gather, rest = rest[:N_GATHER], rest[N_GATHER:]
    sketch_in, local, gram_local, gram, raw, terms, moments, moved, stage, landed, sketch = rest[:11]
    slots, rows_of, factor_work, projected, whole, back, tiles, squares_in = rest[11:19]
    ms, mr, ss, sr, gs, gr, ps, pr, qs, qr, zs, zr, bs, br, slot_pair, sq_pair = rest[19:]
    dp, mp, chip, core = place()
    partner = {"mp": chip * 2 + 1 - core}
    width = og.shape[1]
    barrier, count = greet("all")
    for i in range(DP):
        stop = min(SLICE, width - i * SLICE)
        if stop < SLICE:
            moments[i] = jnp.zeros((32, 2 * SLICE), F32)
        if stop > 0:
            moments[i, :, :stop] = first[:, i * SLICE : i * SLICE + stop]
            moments[i, :, SLICE : SLICE + stop] = second[:, i * SLICE : i * SLICE + stop]
    terms[width // 8 * 8 :, :] = jnp.zeros((WIDE - width // 8 * 8, R), F32)
    factor_work[:, R:] = jnp.where(
        lax.broadcasted_iota(jnp.int32, (R, R), 0) == lax.broadcasted_iota(jnp.int32, (R, R), 1), 1.0, 0.0
    )
    pl.semaphore_wait(barrier, count)

    def in_half(h):
        return jnp.dot(og[half_rows(h), :], tm[...], preferred_element_type=F32)

    sum_in = PlaneSum(in_half, sketch_in, BF16, sums[0])
    sum_in.start()

    def moment_copy(k):
        to = (dp + k) % DP
        return send(moments.at[to], moved.at[dp], ms.at[k - 1], mr.at[k - 1], {"dp": to})

    to_ring(moment_copy)
    moved[dp] = moments[dp]
    sum_in.scatter()
    sum_in.gather()
    sum_in.share()
    near, far = half_rows(core), half_rows(1 - core)
    local[...] = dot_t(act[near, :], sketch_in[near, :]).reshape(DP, 16, R)
    sum_in.end()
    local[...] += dot_t(act[far, :], sketch_in[far, :]).reshape(DP, 16, R)

    stage[...] = local[...].astype(BF16)

    def stage_copy(k):
        to = (dp + k) % DP
        return send(stage.at[to], landed.at[k - 1], ss.at[k - 1], sr.at[k - 1], {"dp": to})

    to_ring(stage_copy)

    def add(k, total):
        stage_copy(k).wait_recv()
        return total + landed[k - 1].astype(F32)

    own = lax.fori_loop(1, DP, add, local[dp]).astype(BF16)
    sketch[dp] = own
    slots[chip, core] = own

    def sketch_copy(k):
        return send(
            sketch.at[dp], sketch.at[dp], gs.at[k - 1], gr.at[k - 1], {"dp": (dp + k) % DP}
        )

    to_ring(sketch_copy)
    slot_gather = plane_gather(slots.at[chip, core], ps, pr)
    slot_half = slots.at[:, core]
    slot_swap = send(slot_half, slot_half, slot_pair.at[0], slot_pair.at[1], partner)
    wait_all(sketch_copy, 1, DP)
    rows_block = sketch[...].reshape(256, R)

    def raw_half(h):
        return jnp.dot(act[half_rows(h), :], rows_block, preferred_element_type=F32)

    def gram_half(h):
        return gram_local[half_rows(h), :]

    sum_raw = PlaneSum(raw_half, raw, BF16, sums[1])
    sum_gram = PlaneSum(gram_half, gram, F32, sums[2])
    sum_raw.start()
    gram_local[...] = dot_t(rows_block, rows_block)
    sum_gram.start()
    sum_raw.scatter()
    sum_gram.scatter()
    sum_raw.gather()
    sum_gram.gather()
    sum_raw.share()
    wait_all(slot_gather, 1, CHIPS)
    slot_swap.start()
    sum_raw.end()

    terms[:width, :] = dot_t(og[...], raw[...])
    fold = FoldedScatter(terms.reshape(DP, SLICE, R), fold_refs)
    fold.start()
    sum_gram.share()
    sum_gram.end()
    factor_work[:, :R] = gram[...]
    invert_factor(factor_work, fold.fold)
    inverse = factor_work[:, R:]
    part = fold.end()
    result = exact_dot(inverse, part, ((1,), (1,)))

    wait_all(moment_copy, 1, DP)
    projected[...] = result.reshape(DP, 32, SLICE)
    both = moved[...].reshape(R, 2 * SLICE)
    new_m = beta_one * both[:, :SLICE] + (1.0 - beta_one) * result
    new_v = beta_two * both[:, SLICE:] + (1.0 - beta_two) * result * result
    correct_one = 1.0 - beta_one**STEP
    correct_two = 1.0 - beta_two**STEP
    direction = new_m / correct_one / (jnp.sqrt(new_v / correct_two) + adam_eps)
    whole[dp] = direction.T.astype(BF16)
    tiles[0] = jnp.broadcast_to(jnp.sum(direction * direction, keepdims=True), (8, 128))
    back[dp] = projected[dp]

    pair_copy = send(tiles.at[0], squares_in.at[0], sq_pair.at[0], sq_pair.at[1], partner)

    def chip_copy(k):
        to = {"mp": chip_at(chip, k) * 2 + core}
        return send(tiles.at[1], squares_in.at[k], qs.at[k - 1], qr.at[k - 1], to)

    def plane_copy(k):
        to = {"dp": (dp + k) % DP}
        return send(tiles.at[2], squares_in.at[15 + k], zs.at[k - 1], zr.at[k - 1], to)

    def back_copy(k):
        to = (dp + k) % DP
        return send(projected.at[to], back.at[dp], bs.at[k - 1], br.at[k - 1], {"dp": to})

    def add_all(copy, base, total):
        def go(k, value):
            copy(k).wait_recv()
            return value + squares_in[base + k]

        return lax.fori_loop(1, 16, go, total)

    def at_start():
        pair_copy.start()
        to_ring(back_copy)
        high = inverse.astype(BF16)
        low = (inverse - high.astype(F32)).astype(BF16)
        slot_swap.wait_recv()
        rows = slots[...].reshape(R, R)
        by_columns = (((1,), (1,)), ((), ()))
        basis = lax.dot_general(rows, high, by_columns, preferred_element_type=F32)
        basis += lax.dot_general(rows, low, by_columns, preferred_element_type=F32)
        rows_of[...] = basis.astype(BF16)

    def after_one():
        pair_copy.wait_recv()
        tiles[1] = tiles[0] + squares_in[0]

        def go(k, _):
            chip_copy(k).start()
            return 0

        lax.fori_loop(1, 16, go, 0)

    def after_three():
        tiles[2] = add_all(chip_copy, 0, tiles[1])
        to_ring(plane_copy)

    def after_five():
        wait_all(back_copy, 1, DP)
        sums_here = jnp.concatenate([back[i] for i in range(DP)], axis=1)[:, :width]
        new_first[...] = beta_one * first[...] + (1.0 - beta_one) * sums_here
        new_second[...] = beta_two * second[...] + (1.0 - beta_two) * sums_here * sums_here

    steps = (at_start, after_one, None, after_three, None, after_five)
    done_gather = Ring.all_gather(whole, gather, SLICE, 2, steps)
    product = lax.dot_general(
        rows_of[...],
        whole[...].reshape(WIDE, R),
        (((1,), (1,)), ((), ())),
        preferred_element_type=F32,
    )
    total_squares = add_all(plane_copy, 15, tiles[2])
    factor = lax.rsqrt(total_squares / (R * FF) + norm_eps)[0:1, 0:1]
    update[...] = (factor * product[:, :width]).astype(BF16)

    for plane in (sum_in, sum_raw, sum_gram):
        plane.drain()
    fold.drain()
    done_gather()
    pair_copy.wait_send()
    slot_swap.wait_send()
    wait_all(slot_gather, 1, CHIPS, recv=False)
    for copy in (stage_copy, sketch_copy, moment_copy, chip_copy, plane_copy, back_copy):
        wait_all(copy, 1, 16, recv=False)


def galore_call(out_grads, test_matrix, activations, first, second):
    return pl.pallas_call(
        galore_kernel,
        out_shape=(
            jax.ShapeDtypeStruct((R, first.shape[1]), BF16),
            jax.ShapeDtypeStruct(first.shape, F32),
            jax.ShapeDtypeStruct(second.shape, F32),
        ),
        in_specs=[VMEM] * 5,
        out_specs=(VMEM,) * 3,
        scratch_shapes=[
            *PlaneSum.scratch(BF16),
            *PlaneSum.scratch(BF16),
            *PlaneSum.scratch(F32),
            *FoldedScatter.scratch(SLICE, R),
            *Ring.scratch_gather(2),
            pltpu.VMEM((R, R), BF16),
            pltpu.VMEM((DP, 16, R), F32),
            pltpu.VMEM((R, R), F32),
            pltpu.VMEM((R, R), F32),
            pltpu.VMEM((R, R), BF16),
            pltpu.VMEM((WIDE, R), F32),
            pltpu.VMEM((DP, 32, 2 * SLICE), F32),
            pltpu.VMEM((DP, 32, 2 * SLICE), F32),
            pltpu.VMEM((DP, 16, R), BF16),
            pltpu.VMEM((DP - 1, 16, R), BF16),
            pltpu.VMEM((DP, 16, R), BF16),
            pltpu.VMEM((CHIPS, 2, 16, R), BF16),
            pltpu.VMEM((R, R), BF16),
            pltpu.VMEM((R, 2 * R), F32),
            pltpu.VMEM((DP, 32, SLICE), F32),
            pltpu.VMEM((DP, SLICE, R), BF16),
            pltpu.VMEM((DP, 32, SLICE), F32),
            pltpu.VMEM((3, 8, 128), F32),
            pltpu.VMEM((31, 8, 128), F32),
            *[sem for _ in range(7) for sem in dp_semaphores()],
            pltpu.SemaphoreType.DMA((2,)),
            pltpu.SemaphoreType.DMA((2,)),
        ],
        compiler_params=pltpu.CompilerParams(
            collective_id=0, has_side_effects=True, vmem_limit_bytes=48 * 2**20
        ),
        name="galore_step",
    )(out_grads, test_matrix, activations, first, second)


def shards(activations, out_grads, test_matrix, first_moment, second_moment):
    update, new_first, new_second = galore_call(
        out_grads, test_matrix, activations, first_moment, second_moment
    )
    return (update.reshape(lax.axis_size("mp"), 16, out_grads.shape[1]), new_first, new_second)


def solution(mesh):
    placed = (P("dp", "mp"), P("dp", "mp"), P("mp", None), P("dp", "mp"), P("dp", "mp"))
    return jax.shard_map(
        shards,
        mesh=mesh,
        in_specs=placed,
        out_specs=(P(None, "dp", "mp"), P("dp", "mp"), P("dp", "mp")),
        check_vma=False,
    )
```

```python
import jax
import jax.numpy as jnp
from jax import lax
from jax.experimental import pallas as pl
from jax.experimental.pallas import tpu as pltpu
from jax.sharding import PartitionSpec as P

FF = 29568
R = 512
STEP = 100

beta_one = 0.9
beta_two = 0.999
adam_eps = 1e-08
norm_eps = 1e-06

MESH = pl.DeviceIdType.MESH
F32 = jnp.float32
BF16 = jnp.bfloat16
CHIPS = 16
DP = 16


def place():
    mp = lax.axis_index("mp")
    core = mp % 2
    chip = mp // 2
    return lax.axis_index("dp"), mp, chip, core


def chip_at(chip, k):
    x = (chip // 4 + k // 4) % 4
    y = (chip % 4 + k % 4) % 4
    return x * 4 + y


def greet(dp_offsets):
    dp, mp, chip, core = place()
    barrier = pltpu.get_barrier_semaphore()
    pl.semaphore_signal(barrier, inc=1, device_id={"mp": chip * 2 + 1 - core}, device_id_type=MESH)

    def to_chip(k, _):
        pl.semaphore_signal(
            barrier, inc=1, device_id={"mp": chip_at(chip, k) * 2 + core}, device_id_type=MESH
        )
        return 0

    lax.fori_loop(1, CHIPS, to_chip, 0)

    def to_ring(k, _):
        pl.semaphore_signal(barrier, inc=1, device_id={"dp": (dp + k) % DP}, device_id_type=MESH)
        return 0

    if dp_offsets == "all":
        lax.fori_loop(1, DP, to_ring, 0)
        return barrier, 1 + (CHIPS - 1) + (DP - 1)
    to_ring(1, 0)
    to_ring(DP - 1, 0)
    return barrier, 1 + (CHIPS - 1) + 2


def send(src, dst, sends, recvs, where):
    return pltpu.make_async_remote_copy(
        src_ref=src, dst_ref=dst, send_sem=sends, recv_sem=recvs, device_id=where, device_id_type=MESH
    )


def plane_scatter(stage, landed, sends, recvs):
    _, _, chip, core = place()

    def copy(k):
        there = chip_at(chip, k)
        return send(
            stage.at[there], landed.at[k - 1], sends.at[k - 1], recvs.at[k - 1], {"mp": there * 2 + core}
        )

    def go(k, _):
        copy(k).start()
        return 0

    lax.fori_loop(1, CHIPS, go, 0)
    return copy


def plane_gather(block, sends, recvs):
    _, _, chip, core = place()

    def copy(k):
        there = chip_at(chip, k)
        return send(block, block, sends.at[k - 1], recvs.at[k - 1], {"mp": there * 2 + core})

    def go(k, _):
        copy(k).start()
        return 0

    lax.fori_loop(1, CHIPS, go, 0)
    return copy


def wait_all(copy, first, last, recv=True):
    def step(k, _):
        if recv:
            copy(k).wait_recv()
        else:
            copy(k).wait_send()
        return 0

    lax.fori_loop(first, last, step, 0)


class PlaneSum:
    COUNT = 9

    def scratch(kind, half=256, width=R):
        return [
            pltpu.VMEM((half, width), kind),
            pltpu.VMEM((half, width), kind),
            pltpu.VMEM((CHIPS, half // CHIPS, width), kind),
            pltpu.VMEM((CHIPS - 1, half // CHIPS, width), kind),
            pltpu.SemaphoreType.DMA((4,)),
            pltpu.SemaphoreType.DMA((CHIPS - 1,)),
            pltpu.SemaphoreType.DMA((CHIPS - 1,)),
            pltpu.SemaphoreType.DMA((CHIPS - 1,)),
            pltpu.SemaphoreType.DMA((CHIPS - 1,)),
        ]

    def __init__(self, half_of, full, kind, refs):
        self.half_of, self.full, self.kind = half_of, full, kind
        self.give, self.take, self.stage, self.landed, pair, self.s1, self.r1, self.s2, self.r2 = refs
        _, _, self.chip, self.core = place()
        partner = {"mp": self.chip * 2 + 1 - self.core}
        self.swap = send(self.give, self.take, pair.at[0], pair.at[1], partner)
        self.rows = full.shape[0] // 2
        half = full.at[half_rows(self.core, self.rows), :]
        self.swap_full = send(half, half, pair.at[2], pair.at[3], partner)

    def fill(self):
        self.give[...] = self.half_of(1 - self.core).astype(self.kind)

    def start(self):
        self.fill()
        self.swap.start()

    def scatter(self):
        own = self.half_of(self.core)
        self.swap.wait_recv()
        both = own + self.take[...].astype(F32)
        self.stage[...] = both.astype(self.kind).reshape(self.stage.shape)
        self.out = plane_scatter(self.stage, self.landed, self.s1, self.r1)

    def gather(self):
        def add(k, total):
            self.out(k).wait_recv()
            return total + self.landed[k - 1].astype(F32)

        total = lax.fori_loop(1, CHIPS, add, self.stage[self.chip].astype(F32))
        count = self.rows // CHIPS
        mine = pl.ds(pl.multiple_of(self.core * self.rows + self.chip * count, count), count)
        self.full[mine, :] = total.astype(self.kind)
        self.back = plane_gather(self.full.at[mine, :], self.s2, self.r2)

    def share(self):
        wait_all(self.back, 1, CHIPS)
        self.swap_full.start()

    def end(self):
        self.swap_full.wait_recv()

    def drain(self):
        self.swap.wait_send()
        wait_all(self.out, 1, CHIPS, recv=False)
        wait_all(self.back, 1, CHIPS, recv=False)
        self.swap_full.wait_send()


def to_ring(copy_to):
    def go(i, _):
        copy_to(8 + (2 * (i % 2) - 1) * ((i + 1) // 2)).start()
        return 0

    lax.fori_loop(0, DP - 1, go, 0)


class FoldedScatter:
    COUNT = 9

    def scratch(rows, width):
        return [
            pltpu.VMEM((4, 3, rows, width), BF16),
            pltpu.VMEM((4, rows, width), BF16),
            pltpu.VMEM((3, rows, width), BF16),
            pltpu.VMEM((rows, width), F32),
            pltpu.SemaphoreType.DMA((4, 3)),
            pltpu.SemaphoreType.DMA((4, 3)),
            pltpu.SemaphoreType.DMA((3,)),
            pltpu.SemaphoreType.DMA((3,)),
            pltpu.VMEM((DP, rows, width), BF16),
        ]

    def __init__(self, local, refs):
        self.local = local
        self.near, self.stage, self.far, self.own, self.ns, self.nr, self.fs, self.fr, self.give = refs
        self.dp = lax.axis_index("dp")
        self.cls, self.row = self.dp % 4, self.dp // 4

    def near_copy(self, o, j):
        q = (self.row + o) % 4
        step = (1, DP - 1, DP - 2 + 4 * (q % 2))[j]
        to = (self.dp + step) % DP
        return send(
            self.give.at[to % 4 + 4 * q], self.near.at[q, j], self.ns.at[q, j], self.nr.at[q, j], {"dp": to}
        )

    def far_copy(self, o):
        q = (self.row + o) % 4
        return send(
            self.stage.at[q], self.far.at[o - 1], self.fs.at[o - 1], self.fr.at[o - 1],
            {"dp": self.cls + 4 * q},
        )

    def start(self):
        for b in range(DP):
            self.give[b] = self.local(b).astype(BF16)
        for o in (2, 1, 3, 0):
            for j in range(3):
                self.near_copy(o, j).start()

    def fold(self):
        for o in (2, 1, 3, 0):
            q = (self.row + o) % 4
            total = self.local(self.cls + 4 * q)
            for j in range(3):
                self.near_copy(o, j).wait_recv()
                total = total + self.near[q, j].astype(F32)
            if o:
                self.stage[q] = total.astype(BF16)
                self.far_copy(o).start()
            else:
                self.own[...] = total

    def end(self):
        total = self.own[...]
        for o in (1, 3, 2):
            self.far_copy(o).wait_recv()
            total = total + self.far[o - 1].astype(F32)
        return total

    def drain(self):
        for o in range(4):
            for j in range(3):
                self.near_copy(o, j).wait_send()
            if o:
                self.far_copy(o).wait_send()


class FoldedGather:
    COUNT = 4

    def scratch():
        return [
            pltpu.SemaphoreType.DMA((3,)),
            pltpu.SemaphoreType.DMA((3,)),
            pltpu.SemaphoreType.DMA((4, 3)),
            pltpu.SemaphoreType.DMA((4, 3)),
        ]

    def __init__(self, whole, refs):
        self.whole = whole
        self.fs, self.fr, self.ns, self.nr = refs
        self.dp = lax.axis_index("dp")
        self.cls, self.row = self.dp % 4, self.dp // 4

    def far_copy(self, o):
        own = self.whole.at[self.dp]
        to = self.cls + 4 * ((self.row + o) % 4)
        return send(own, own, self.fs.at[o - 1], self.fr.at[o - 1], {"dp": to})

    def near_copy(self, q, j):
        block = self.whole.at[self.cls + 4 * q]
        step = (1, DP - 1, 2 + (DP - 4) * (q % 2))[j]
        return send(
            block, block, self.ns.at[q, j], self.nr.at[q, j], {"dp": (self.dp + step) % DP}
        )

    def start(self):
        for o in (2, 1, 3):
            self.far_copy(o).start()
        for j in range(3):
            self.near_copy(self.row, j).start()

    def forward(self):
        for o in (1, 3, 2):
            self.far_copy(o).wait_recv()
            for j in range(3):
                self.near_copy((self.row + 4 - o) % 4, j).start()

    def end(self):
        for q in range(4):
            for j in range(3):
                self.near_copy(q, j).wait_recv()

    def drain(self):
        for o in range(1, 4):
            self.far_copy(o).wait_send()
        for q in range(4):
            for j in range(3):
                self.near_copy(q, j).wait_send()


def half_rows(h, count=256):
    return pl.ds(pl.multiple_of(h * count, count), count)


def dot_t(a, b):
    return lax.dot_general(a, b, (((0,), (0,)), ((), ())), preferred_element_type=F32)


LEAF = 128


def exact_dot(a, b, dims):
    return lax.dot_general(
        a, b, (dims, ((), ())), precision=lax.Precision.HIGHEST, preferred_element_type=F32
    )


def leaf_inverse(block, inverse):
    groups = LEAF // 8
    sub = lax.broadcasted_iota(jnp.int32, (8, 128), 0)

    def spread(row):
        return jnp.broadcast_to(row, (8, 128))

    for p in range(groups):
        cols = {
            g: [spread(block[g][:, 8 * p + j : 8 * p + j + 1]) for j in range(8)]
            for g in range(p, groups)
        }
        pivots = jnp.zeros((8, 128), F32)
        for j in range(8):
            pivot = spread(cols[p][j][j : j + 1, :])
            over = 1.0 / pivot
            pivots = jnp.where(sub == j, pivot, pivots)
            below = jnp.where(sub > j, cols[p][j], 0.0)
            row_block = spread(block[p][j : j + 1, :]) * over
            row_inverse = spread(inverse[p][j : j + 1, :]) * over
            ratio = {i: spread(cols[p][j][i : i + 1, :]) * over for i in range(j + 1, 8)}
            for g in range(p, groups):
                left = below if g == p else cols[g][j]
                for i in range(j + 1, 8):
                    cols[g][i] = cols[g][i] - left * ratio[i]
                block[g] = block[g] - left * row_block
                inverse[g] = inverse[g] - left * row_inverse
        inverse[p] = inverse[p] * lax.rsqrt(pivots)
    return jnp.concatenate(inverse, axis=0)


VMEM = pl.BlockSpec(memory_space=pltpu.VMEM)


N_PLANE = PlaneSum.COUNT
N_FOLD = FoldedScatter.COUNT
N_GATHER = FoldedGather.COUNT
SLICE = 64
WIDE = DP * SLICE
HALF = R // 2
LEAVES = R // LEAF
UPPER = [(i, j) for i in range(LEAVES) for j in range(i, LEAVES)]
PACKED = len(UPPER) * LEAF


def dp_semaphores():
    return [pltpu.SemaphoreType.DMA((DP - 1,)) for _ in range(2)]


def eliminate(work, k):
    lane = lax.broadcasted_iota(jnp.int32, (8, 128), 1)
    sub = lax.broadcasted_iota(jnp.int32, (8, 128), 0)
    here, after = k * LEAF, (k + 1) * LEAF
    tail = R - after
    block = [work[here + 8 * g : here + 8 * g + 8, here:after] for g in range(LEAF // 8)]
    unit = [jnp.where(lane == sub + 8 * g, 1.0, 0.0) for g in range(LEAF // 8)]
    inverse = leaf_inverse(block, unit)
    panel = exact_dot(inverse, work[here:after, after : R + here], ((1,), (0,)))
    panel = jnp.concatenate([panel, inverse], axis=1)
    work[here:after, R : R + after] = panel[:, tail:]
    if tail:
        work[after:, after : R + after] -= exact_dot(panel[:, :tail], panel, ((0,), (0,)))


def galore_kernel(ogt_in, tm_in, act_in, first_in, second_in, update, sums_out, *refs):
    sums = [refs[i * N_PLANE : (i + 1) * N_PLANE] for i in range(3)]
    rest = refs[3 * N_PLANE :]
    fold_refs, rest = (rest[:N_FOLD], rest[N_FOLD : 2 * N_FOLD]), rest[2 * N_FOLD :]
    gather_refs, rest = (rest[:N_GATHER], rest[N_GATHER : 2 * N_GATHER]), rest[2 * N_GATHER :]
    sketch_in, local, gram_local, gram, raw, terms, moments, moved, stage, landed, sketch = rest[:11]
    slots, rows_of, work, projected, whole_one, whole_two, back, tiles, squares_in = rest[11:20]
    ms, mr, ss, sr, gs, gr, ps, pr, qs, qr, zs, zr, bs, br, slot_pair, sq_pair = rest[20:36]
    ogt, tm, act, first, second, load_sems = rest[36:]
    dp, mp, chip, core = place()
    partner = {"mp": chip * 2 + 1 - core}
    width = ogt.shape[0]
    pairs = ((ogt_in, ogt), (tm_in, tm), (act_in, act), (first_in, first), (second_in, second))
    loads = [pltpu.make_async_copy(a, b, load_sems.at[i]) for i, (a, b) in enumerate(pairs)]
    for load in loads:
        load.start()
    barrier, count = greet("all")
    loads[0].wait()
    loads[1].wait()

    def in_half(h):
        return dot_t(ogt[:, half_rows(h)], tm[...])

    sum_in = PlaneSum(in_half, sketch_in, BF16, sums[0])
    sum_in.fill()
    pl.semaphore_wait(barrier, count)
    sum_in.swap.start()

    def moment_copy(k):
        to = (dp + k) % DP
        return send(moments.at[to], moved.at[dp], ms.at[k - 1], mr.at[k - 1], {"dp": to})

    sum_in.scatter()
    loads[3].wait()
    loads[4].wait()
    for i in range(DP):
        stop = min(SLICE, width - i * SLICE)
        if stop < SLICE:
            moments[i] = jnp.zeros((32, 2 * SLICE), F32)
        if stop > 0:
            moments[i, :, :stop] = first[:, i * SLICE : i * SLICE + stop]
            moments[i, :, SLICE : SLICE + stop] = second[:, i * SLICE : i * SLICE + stop]
    to_ring(moment_copy)
    moved[dp] = moments[dp]
    sum_in.gather()
    terms[width // 8 * 8 :, :] = jnp.zeros((WIDE - width // 8 * 8, R), F32)
    work[:, R:] = jnp.zeros((R, R), F32)
    sum_in.share()
    loads[2].wait()
    near, far = half_rows(core), half_rows(1 - core)
    local[...] = dot_t(act[near, :], sketch_in[near, :]).reshape(DP, 16, R)
    sum_in.end()
    local[...] += dot_t(act[far, :], sketch_in[far, :]).reshape(DP, 16, R)

    stage[...] = local[...].astype(BF16)

    def stage_copy(k):
        to = (dp + k) % DP
        return send(stage.at[to], landed.at[k - 1], ss.at[k - 1], sr.at[k - 1], {"dp": to})

    to_ring(stage_copy)

    def add(k, total):
        stage_copy(k).wait_recv()
        return total + landed[k - 1].astype(F32)

    own = lax.fori_loop(1, DP, add, local[dp]).astype(BF16)
    sketch[dp] = own
    slots[chip, core] = own

    def sketch_copy(k):
        return send(
            sketch.at[dp], sketch.at[dp], gs.at[k - 1], gr.at[k - 1], {"dp": (dp + k) % DP}
        )

    to_ring(sketch_copy)
    slot_gather = plane_gather(slots.at[chip, core], ps, pr)
    slot_half = slots.at[:, core]
    slot_swap = send(slot_half, slot_half, slot_pair.at[0], slot_pair.at[1], partner)
    wait_all(sketch_copy, 1, DP)
    rows_block = sketch[...].reshape(256, R)

    def raw_half(h):
        return jnp.dot(act[half_rows(h), :], rows_block, preferred_element_type=F32)

    def gram_half(h):
        return gram_local[half_rows(h, PACKED // 2), :]

    sum_raw = PlaneSum(raw_half, raw, BF16, sums[1])
    sum_gram = PlaneSum(gram_half, gram, F32, sums[2])
    sum_raw.start()
    for i in range(LEAVES):
        row = dot_t(rows_block[:, i * LEAF : (i + 1) * LEAF], rows_block[:, i * LEAF :])
        for j in range(i, LEAVES):
            at = UPPER.index((i, j)) * LEAF
            gram_local[at : at + LEAF, :] = row[:, (j - i) * LEAF : (j - i + 1) * LEAF]
    sum_gram.start()
    sum_raw.scatter()
    sum_gram.scatter()
    sum_raw.gather()
    sum_gram.gather()
    sum_raw.share()
    wait_all(slot_gather, 1, CHIPS)
    slot_swap.start()
    sum_raw.end()

    terms[:width, :] = jnp.dot(ogt[...], raw[...], preferred_element_type=F32)

    def terms_of(columns):
        def block(b):
            if isinstance(b, int):
                return terms[b * SLICE : (b + 1) * SLICE, columns]
            return terms[pl.ds(pl.multiple_of(b * SLICE, SLICE), SLICE), columns]

        return block

    fold_one = FoldedScatter(terms_of(slice(0, HALF)), fold_refs[0])
    fold_two = FoldedScatter(terms_of(slice(HALF, R)), fold_refs[1])
    fold_one.start()
    sum_gram.share()
    fold_two.start()
    sum_gram.end()
    for n, (i, j) in enumerate(UPPER):
        work[i * LEAF : (i + 1) * LEAF, j * LEAF : (j + 1) * LEAF] = gram[n * LEAF : (n + 1) * LEAF, :]

    def adam(h, result, whole):
        by_owner = result.reshape(8, 2, 16, SLICE)
        projected[8 * h : 8 * h + 8] = jnp.concatenate([by_owner[:, 0], by_owner[:, 1]], axis=2)
        both = moved[8 * h : 8 * h + 8].reshape(HALF, 2 * SLICE)
        new_m = beta_one * both[:, :SLICE] + (1.0 - beta_one) * result
        new_v = beta_two * both[:, SLICE:] + (1.0 - beta_two) * result * result
        correct_one = 1.0 - beta_one**STEP
        correct_two = 1.0 - beta_two**STEP
        direction = new_m / correct_one / (jnp.sqrt(new_v / correct_two) + adam_eps)
        whole[dp] = direction.T.astype(BF16)
        return jnp.sum(direction * direction, keepdims=True)

    gather_one = FoldedGather(whole_one, gather_refs[0])
    gather_two = FoldedGather(whole_two, gather_refs[1])
    by_columns = (((1,), (1,)), ((), ()))

    def basis_columns(k):
        here, after = k * LEAF, (k + 1) * LEAF
        inverse = work[here:after, R : R + after]
        high = inverse.astype(BF16)
        low = (inverse - high.astype(F32)).astype(BF16)
        rows = slots[...].reshape(R, R)[:, :after]
        columns = lax.dot_general(rows, high, by_columns, preferred_element_type=F32)
        columns += lax.dot_general(rows, low, by_columns, preferred_element_type=F32)
        rows_of[:, here:after] = columns.astype(BF16)

    def ring_copy(k):
        to = {"dp": (dp + k) % DP}
        return send(tiles.at[0], squares_in.at[15 + k], zs.at[k - 1], zr.at[k - 1], to)

    pair_copy = send(tiles.at[1], squares_in.at[0], sq_pair.at[0], sq_pair.at[1], partner)

    def chip_copy(k):
        to = {"mp": chip_at(chip, k) * 2 + core}
        return send(tiles.at[2], squares_in.at[k], qs.at[k - 1], qr.at[k - 1], to)

    def back_copy(k):
        to = (dp + k) % DP
        return send(projected.at[to], back.at[dp], bs.at[k - 1], br.at[k - 1], {"dp": to})

    def back_start(h):
        def go(k, _):
            @pl.when((dp + k) % DP // (DP // 2) == h)
            def _():
                back_copy(k).start()

            return 0

        lax.fori_loop(1, DP, go, 0)

    def add_all(copy, base, total):
        def go(k, value):
            copy(k).wait_recv()
            return value + squares_in[base + k]

        return lax.fori_loop(1, 16, go, total)

    eliminate(work, 0)
    fold_one.fold()
    eliminate(work, 1)
    fold_two.fold()
    eliminate(work, 2)
    slot_swap.wait_recv()
    for k in range(LEAVES - 1):
        basis_columns(k)
    for plane in (sum_in, sum_raw, sum_gram):
        plane.drain()
    slot_swap.wait_send()
    wait_all(slot_gather, 1, CHIPS, recv=False)
    for copy in (stage_copy, sketch_copy, moment_copy):
        wait_all(copy, 1, DP, recv=False)
    wait_all(moment_copy, 1, DP)
    part_one = fold_one.end()
    squares = adam(0, exact_dot(work[:HALF, R : R + HALF], part_one, ((1,), (1,))), whole_one)
    gather_one.start()
    back_start(0)
    eliminate(work, LEAVES - 1)
    basis_columns(LEAVES - 1)
    result = exact_dot(work[HALF:, R : R + HALF], part_one, ((1,), (1,)))
    part_two = fold_two.end()
    result += exact_dot(work[HALF:, R + HALF :], part_two, ((1,), (1,)))
    squares += adam(1, result, whole_two)
    tiles[0] = jnp.broadcast_to(squares, (8, 128))
    to_ring(ring_copy)
    gather_two.start()
    back_start(1)
    back[dp] = projected[dp]
    gather_one.forward()
    fold_one.drain()
    fold_two.drain()
    tiles[1] = add_all(ring_copy, 15, tiles[0])
    pair_copy.start()
    gather_two.forward()
    pair_copy.wait_recv()
    tiles[2] = tiles[1] + squares_in[0]

    def chip_start(k, _):
        chip_copy(k).start()
        return 0

    lax.fori_loop(1, CHIPS, chip_start, 0)
    gather_one.end()

    def product_of(columns, whole):
        return lax.dot_general(
            rows_of[:, columns],
            whole[...].reshape(WIDE, HALF),
            by_columns,
            preferred_element_type=F32,
        )

    product = product_of(slice(0, HALF), whole_one)
    wait_all(back_copy, 1, DP)
    for r in range(2):
        rows = [back[i, :, r * SLICE : (r + 1) * SLICE] for i in range(DP)]
        sums_out[16 * r : 16 * r + 16, :] = jnp.concatenate(rows, axis=1)[:, :width]
    total_squares = add_all(chip_copy, 0, tiles[2])
    factor = lax.rsqrt(total_squares / (R * FF) + norm_eps)[0:1, 0:1]
    for copy in (ring_copy, back_copy, chip_copy):
        wait_all(copy, 1, 16, recv=False)
    pair_copy.wait_send()
    gather_one.drain()
    gather_two.end()
    product += product_of(slice(HALF, R), whole_two)
    update[...] = (factor * product[:, :width]).astype(BF16)
    gather_two.drain()


def galore_call(out_grads, test_matrix, activations, first, second):
    return pl.pallas_call(
        galore_kernel,
        out_shape=(
            jax.ShapeDtypeStruct((R, first.shape[1]), BF16),
            jax.ShapeDtypeStruct(first.shape, F32),
        ),
        in_specs=[pl.BlockSpec(memory_space=pltpu.HBM)] * 5,
        out_specs=(VMEM,) * 2,
        scratch_shapes=[
            *PlaneSum.scratch(BF16),
            *PlaneSum.scratch(BF16),
            *PlaneSum.scratch(F32, PACKED // 2, LEAF),
            *FoldedScatter.scratch(SLICE, HALF),
            *FoldedScatter.scratch(SLICE, HALF),
            *FoldedGather.scratch(),
            *FoldedGather.scratch(),
            pltpu.VMEM((R, R), BF16),
            pltpu.VMEM((DP, 16, R), F32),
            pltpu.VMEM((PACKED, LEAF), F32),
            pltpu.VMEM((PACKED, LEAF), F32),
            pltpu.VMEM((R, R), BF16),
            pltpu.VMEM((WIDE, R), F32),
            pltpu.VMEM((DP, 32, 2 * SLICE), F32),
            pltpu.VMEM((DP, 32, 2 * SLICE), F32),
            pltpu.VMEM((DP, 16, R), BF16),
            pltpu.VMEM((DP - 1, 16, R), BF16),
            pltpu.VMEM((DP, 16, R), BF16),
            pltpu.VMEM((CHIPS, 2, 16, R), BF16),
            pltpu.VMEM((R, R), BF16),
            pltpu.VMEM((R, 2 * R), F32),
            pltpu.VMEM((DP, 16, 2 * SLICE), F32),
            pltpu.VMEM((DP, SLICE, HALF), BF16),
            pltpu.VMEM((DP, SLICE, HALF), BF16),
            pltpu.VMEM((DP, 16, 2 * SLICE), F32),
            pltpu.VMEM((3, 8, 128), F32),
            pltpu.VMEM((31, 8, 128), F32),
            *[sem for _ in range(7) for sem in dp_semaphores()],
            pltpu.SemaphoreType.DMA((2,)),
            pltpu.SemaphoreType.DMA((2,)),
            pltpu.VMEM(out_grads.shape[::-1], BF16),
            pltpu.VMEM(test_matrix.shape, BF16),
            pltpu.VMEM(activations.shape, BF16),
            pltpu.VMEM(first.shape, F32),
            pltpu.VMEM(second.shape, F32),
            pltpu.SemaphoreType.DMA((5,)),
        ],
        compiler_params=pltpu.CompilerParams(
            collective_id=0, has_side_effects=True, vmem_limit_bytes=60 * 2**20
        ),
        name="galore_step",
    )(out_grads.T, test_matrix, activations, first, second)


def shards(activations, out_grads, test_matrix, first_moment, second_moment):
    update, projected = galore_call(
        out_grads, test_matrix, activations, first_moment, second_moment
    )
    new_first = beta_one * first_moment + (1.0 - beta_one) * projected
    new_second = beta_two * second_moment + (1.0 - beta_two) * projected * projected
    return (update.reshape(lax.axis_size("mp"), 16, out_grads.shape[1]), new_first, new_second)


def solution(mesh):
    placed = (P("dp", "mp"), P("dp", "mp"), P("mp", None), P("dp", "mp"), P("dp", "mp"))
    return jax.shard_map(
        shards,
        mesh=mesh,
        in_specs=placed,
        out_specs=(P(None, "dp", "mp"), P("dp", "mp"), P("dp", "mp")),
        check_vma=False,
    )
```

```python
import jax
import jax.numpy as jnp
from jax import lax
from jax.experimental import pallas as pl
from jax.experimental.pallas import tpu as pltpu
from jax.sharding import PartitionSpec as P

FF = 29568
R = 512
STEP = 100

beta_one = 0.9
beta_two = 0.999
adam_eps = 1e-08
norm_eps = 1e-06

MESH = pl.DeviceIdType.MESH
F32 = jnp.float32
BF16 = jnp.bfloat16
CHIPS = 16
DP = 16


def place():
    mp = lax.axis_index("mp")
    core = mp % 2
    chip = mp // 2
    return lax.axis_index("dp"), mp, chip, core


def chip_at(chip, k):
    x = (chip // 4 + k // 4) % 4
    y = (chip % 4 + k % 4) % 4
    return x * 4 + y


def greet(dp_offsets):
    dp, mp, chip, core = place()
    barrier = pltpu.get_barrier_semaphore()
    pl.semaphore_signal(barrier, inc=1, device_id={"mp": chip * 2 + 1 - core}, device_id_type=MESH)

    def to_chip(k, _):
        pl.semaphore_signal(
            barrier, inc=1, device_id={"mp": chip_at(chip, k) * 2 + core}, device_id_type=MESH
        )
        return 0

    lax.fori_loop(1, CHIPS, to_chip, 0)

    def to_ring(k, _):
        pl.semaphore_signal(barrier, inc=1, device_id={"dp": (dp + k) % DP}, device_id_type=MESH)
        return 0

    if dp_offsets == "all":
        lax.fori_loop(1, DP, to_ring, 0)
        return barrier, 1 + (CHIPS - 1) + (DP - 1)
    to_ring(1, 0)
    to_ring(DP - 1, 0)
    return barrier, 1 + (CHIPS - 1) + 2


def send(src, dst, sends, recvs, where):
    return pltpu.make_async_remote_copy(
        src_ref=src, dst_ref=dst, send_sem=sends, recv_sem=recvs, device_id=where, device_id_type=MESH
    )


def plane_scatter(stage, landed, sends, recvs):
    _, _, chip, core = place()

    def copy(k):
        there = chip_at(chip, k)
        return send(
            stage.at[there], landed.at[k - 1], sends.at[k - 1], recvs.at[k - 1], {"mp": there * 2 + core}
        )

    def go(k, _):
        copy(k).start()
        return 0

    lax.fori_loop(1, CHIPS, go, 0)
    return copy


def plane_gather(block, sends, recvs):
    _, _, chip, core = place()

    def copy(k):
        there = chip_at(chip, k)
        return send(block, block, sends.at[k - 1], recvs.at[k - 1], {"mp": there * 2 + core})

    def go(k, _):
        copy(k).start()
        return 0

    lax.fori_loop(1, CHIPS, go, 0)
    return copy


def wait_all(copy, first, last, recv=True):
    def step(k, _):
        if recv:
            copy(k).wait_recv()
        else:
            copy(k).wait_send()
        return 0

    lax.fori_loop(first, last, step, 0)


class PlaneSum:
    COUNT = 9

    def scratch(kind, half=256, width=R):
        return [
            pltpu.VMEM((half, width), kind),
            pltpu.VMEM((half, width), kind),
            pltpu.VMEM((CHIPS, half // CHIPS, width), kind),
            pltpu.VMEM((CHIPS - 1, half // CHIPS, width), kind),
            pltpu.SemaphoreType.DMA((4,)),
            pltpu.SemaphoreType.DMA((CHIPS - 1,)),
            pltpu.SemaphoreType.DMA((CHIPS - 1,)),
            pltpu.SemaphoreType.DMA((CHIPS - 1,)),
            pltpu.SemaphoreType.DMA((CHIPS - 1,)),
        ]

    def __init__(self, half_of, full, kind, refs):
        self.half_of, self.full, self.kind = half_of, full, kind
        self.give, self.take, self.stage, self.landed, pair, self.s1, self.r1, self.s2, self.r2 = refs
        _, _, self.chip, self.core = place()
        partner = {"mp": self.chip * 2 + 1 - self.core}
        self.swap = send(self.give, self.take, pair.at[0], pair.at[1], partner)
        self.rows = full.shape[0] // 2
        half = full.at[half_rows(self.core, self.rows), :]
        self.swap_full = send(half, half, pair.at[2], pair.at[3], partner)

    def fill(self):
        self.give[...] = self.half_of(1 - self.core).astype(self.kind)

    def start(self):
        self.fill()
        self.swap.start()

    def scatter(self):
        own = self.half_of(self.core)
        self.swap.wait_recv()
        both = own + self.take[...].astype(F32)
        self.stage[...] = both.astype(self.kind).reshape(self.stage.shape)
        self.out = plane_scatter(self.stage, self.landed, self.s1, self.r1)

    def gather(self):
        def add(k, total):
            self.out(k).wait_recv()
            return total + self.landed[k - 1].astype(F32)

        total = lax.fori_loop(1, CHIPS, add, self.stage[self.chip].astype(F32))
        count = self.rows // CHIPS
        mine = pl.ds(pl.multiple_of(self.core * self.rows + self.chip * count, count), count)
        self.full[mine, :] = total.astype(self.kind)
        self.back = plane_gather(self.full.at[mine, :], self.s2, self.r2)

    def share(self):
        wait_all(self.back, 1, CHIPS)
        self.swap_full.start()

    def end(self):
        self.swap_full.wait_recv()

    def drain(self):
        self.swap.wait_send()
        wait_all(self.out, 1, CHIPS, recv=False)
        wait_all(self.back, 1, CHIPS, recv=False)
        self.swap_full.wait_send()


def to_ring(copy_to):
    def go(i, _):
        copy_to(8 + (2 * (i % 2) - 1) * ((i + 1) // 2)).start()
        return 0

    lax.fori_loop(0, DP - 1, go, 0)


class FoldedScatter:
    COUNT = 9

    def scratch(rows, width):
        return [
            pltpu.VMEM((4, 3, rows, width), BF16),
            pltpu.VMEM((4, rows, width), BF16),
            pltpu.VMEM((3, rows, width), BF16),
            pltpu.VMEM((rows, width), F32),
            pltpu.SemaphoreType.DMA((4, 3)),
            pltpu.SemaphoreType.DMA((4, 3)),
            pltpu.SemaphoreType.DMA((3,)),
            pltpu.SemaphoreType.DMA((3,)),
            pltpu.VMEM((DP, rows, width), BF16),
        ]

    def __init__(self, local, refs):
        self.local = local
        self.near, self.stage, self.far, self.own, self.ns, self.nr, self.fs, self.fr, self.give = refs
        self.dp = lax.axis_index("dp")
        self.cls, self.row = self.dp % 4, self.dp // 4

    def near_copy(self, o, j):
        q = (self.row + o) % 4
        step = (1, DP - 1, DP - 2 + 4 * (q % 2))[j]
        to = (self.dp + step) % DP
        return send(
            self.give.at[to % 4 + 4 * q], self.near.at[q, j], self.ns.at[q, j], self.nr.at[q, j], {"dp": to}
        )

    def far_copy(self, o):
        q = (self.row + o) % 4
        return send(
            self.stage.at[q], self.far.at[o - 1], self.fs.at[o - 1], self.fr.at[o - 1],
            {"dp": self.cls + 4 * q},
        )

    def start(self):
        for b in range(DP):
            self.give[b] = self.local(b).astype(BF16)
        for o in (2, 1, 3, 0):
            for j in range(3):
                self.near_copy(o, j).start()

    def fold(self):
        for o in (2, 1, 3, 0):
            q = (self.row + o) % 4
            total = self.local(self.cls + 4 * q)
            for j in range(3):
                self.near_copy(o, j).wait_recv()
                total = total + self.near[q, j].astype(F32)
            if o:
                self.stage[q] = total.astype(BF16)
                self.far_copy(o).start()
            else:
                self.own[...] = total

    def end(self):
        total = self.own[...]
        for o in (1, 3, 2):
            self.far_copy(o).wait_recv()
            total = total + self.far[o - 1].astype(F32)
        return total

    def drain(self):
        for o in range(4):
            for j in range(3):
                self.near_copy(o, j).wait_send()
            if o:
                self.far_copy(o).wait_send()


class FoldedGather:
    COUNT = 4

    def scratch():
        return [
            pltpu.SemaphoreType.DMA((3,)),
            pltpu.SemaphoreType.DMA((3,)),
            pltpu.SemaphoreType.DMA((4, 3)),
            pltpu.SemaphoreType.DMA((4, 3)),
        ]

    def __init__(self, whole, refs):
        self.whole = whole
        self.fs, self.fr, self.ns, self.nr = refs
        self.dp = lax.axis_index("dp")
        self.cls, self.row = self.dp % 4, self.dp // 4

    def far_copy(self, o):
        own = self.whole.at[self.dp]
        to = self.cls + 4 * ((self.row + o) % 4)
        return send(own, own, self.fs.at[o - 1], self.fr.at[o - 1], {"dp": to})

    def near_copy(self, q, j):
        block = self.whole.at[self.cls + 4 * q]
        step = (1, DP - 1, 2 + (DP - 4) * (q % 2))[j]
        return send(
            block, block, self.ns.at[q, j], self.nr.at[q, j], {"dp": (self.dp + step) % DP}
        )

    def start(self):
        for o in (2, 1, 3):
            self.far_copy(o).start()
        for j in range(3):
            self.near_copy(self.row, j).start()

    def forward(self):
        for o in (1, 3, 2):
            self.far_copy(o).wait_recv()
            for j in range(3):
                self.near_copy((self.row + 4 - o) % 4, j).start()

    def end(self):
        for q in range(4):
            for j in range(3):
                self.near_copy(q, j).wait_recv()

    def drain(self):
        for o in range(1, 4):
            self.far_copy(o).wait_send()
        for q in range(4):
            for j in range(3):
                self.near_copy(q, j).wait_send()


def half_rows(h, count=256):
    return pl.ds(pl.multiple_of(h * count, count), count)


def dot_t(a, b):
    return lax.dot_general(a, b, (((0,), (0,)), ((), ())), preferred_element_type=F32)


LEAF = 128


def exact_dot(a, b, dims):
    return lax.dot_general(
        a, b, (dims, ((), ())), precision=lax.Precision.HIGHEST, preferred_element_type=F32
    )


def leaf_inverse(block, inverse):
    groups = LEAF // 8
    sub = lax.broadcasted_iota(jnp.int32, (8, 128), 0)

    def spread(row):
        return jnp.broadcast_to(row, (8, 128))

    for p in range(groups):
        cols = {
            g: [spread(block[g][:, 8 * p + j : 8 * p + j + 1]) for j in range(8)]
            for g in range(p, groups)
        }
        pivots = jnp.zeros((8, 128), F32)
        for j in range(8):
            pivot = spread(cols[p][j][j : j + 1, :])
            over = 1.0 / pivot
            pivots = jnp.where(sub == j, pivot, pivots)
            below = jnp.where(sub > j, cols[p][j], 0.0)
            row_block = spread(block[p][j : j + 1, :]) * over
            row_inverse = spread(inverse[p][j : j + 1, :]) * over
            ratio = {i: spread(cols[p][j][i : i + 1, :]) * over for i in range(j + 1, 8)}
            for g in range(p, groups):
                left = below if g == p else cols[g][j]
                for i in range(j + 1, 8):
                    cols[g][i] = cols[g][i] - left * ratio[i]
                block[g] = block[g] - left * row_block
                inverse[g] = inverse[g] - left * row_inverse
        inverse[p] = inverse[p] * lax.rsqrt(pivots)
    return jnp.concatenate(inverse, axis=0)


VMEM = pl.BlockSpec(memory_space=pltpu.VMEM)


N_PLANE = PlaneSum.COUNT
N_FOLD = FoldedScatter.COUNT
N_GATHER = FoldedGather.COUNT
SLICE = 64
WIDE = DP * SLICE
FIRST = 3 * R // 4
AHEAD = FIRST // 32
LEAVES = R // LEAF
UPPER = [(i, j) for i in range(LEAVES) for j in range(i, LEAVES)]
PACKED = len(UPPER) * LEAF


def dp_semaphores():
    return [pltpu.SemaphoreType.DMA((DP - 1,)) for _ in range(2)]


def eliminate(work, k):
    lane = lax.broadcasted_iota(jnp.int32, (8, 128), 1)
    sub = lax.broadcasted_iota(jnp.int32, (8, 128), 0)
    here, after = k * LEAF, (k + 1) * LEAF
    tail = R - after
    block = [work[here + 8 * g : here + 8 * g + 8, here:after] for g in range(LEAF // 8)]
    unit = [jnp.where(lane == sub + 8 * g, 1.0, 0.0) for g in range(LEAF // 8)]
    inverse = leaf_inverse(block, unit)
    panel = exact_dot(inverse, work[here:after, after : R + here], ((1,), (0,)))
    panel = jnp.concatenate([panel, inverse], axis=1)
    work[here:after, R : R + after] = panel[:, tail:]
    if tail:
        work[after:, after : R + after] -= exact_dot(panel[:, :tail], panel, ((0,), (0,)))


def galore_kernel(ogt_in, tm_in, act_in, first_in, second_in, update, sums_out, *refs):
    sums = [refs[i * N_PLANE : (i + 1) * N_PLANE] for i in range(3)]
    rest = refs[3 * N_PLANE :]
    fold_refs, rest = (rest[:N_FOLD], rest[N_FOLD : 2 * N_FOLD]), rest[2 * N_FOLD :]
    gather_refs, rest = (rest[:N_GATHER], rest[N_GATHER : 2 * N_GATHER]), rest[2 * N_GATHER :]
    sketch_in, local, gram_local, gram, raw, terms, moments, moved, stage, landed, sketch = rest[:11]
    slots, rows_of, work, projected, whole_one, whole_two, back, tiles, squares_in = rest[11:20]
    ms, mr, ss, sr, gs, gr, ps, pr, qs, qr, zs, zr, bs, br, slot_pair, sq_pair = rest[20:36]
    ogt, tm, act, first, second, load_sems = rest[36:]
    dp, mp, chip, core = place()
    partner = {"mp": chip * 2 + 1 - core}
    width = ogt.shape[0]
    pairs = ((ogt_in, ogt), (tm_in, tm), (act_in, act), (first_in, first), (second_in, second))
    loads = [pltpu.make_async_copy(a, b, load_sems.at[i]) for i, (a, b) in enumerate(pairs)]
    for load in loads:
        load.start()
    barrier, count = greet("all")
    loads[0].wait()
    loads[1].wait()

    def in_half(h):
        return dot_t(ogt[:, half_rows(h)], tm[...])

    sum_in = PlaneSum(in_half, sketch_in, BF16, sums[0])
    sum_in.fill()
    loads[3].wait()
    loads[4].wait()
    for i in range(DP):
        stop = min(SLICE, width - i * SLICE)
        if stop < SLICE:
            moments[i] = jnp.zeros((32, 2 * SLICE), BF16)
        if stop > 0:
            moments[i, :, :stop] = first[:, i * SLICE : i * SLICE + stop].astype(BF16)
            moments[i, :, SLICE : SLICE + stop] = second[:, i * SLICE : i * SLICE + stop].astype(BF16)
    pl.semaphore_wait(barrier, count)
    sum_in.swap.start()

    def moment_copy(k):
        to = (dp + k) % DP
        return send(moments.at[to], moved.at[dp], ms.at[k - 1], mr.at[k - 1], {"dp": to})

    to_ring(moment_copy)
    sum_in.scatter()
    moved[dp] = moments[dp]
    sum_in.gather()
    terms[width // 8 * 8 :, :] = jnp.zeros((WIDE - width // 8 * 8, R), F32)
    work[:, R:] = jnp.zeros((R, R), F32)
    sum_in.share()
    loads[2].wait()
    near, far = half_rows(core), half_rows(1 - core)
    local[...] = dot_t(act[near, :], sketch_in[near, :]).reshape(DP, 16, R)
    sum_in.end()
    local[...] += dot_t(act[far, :], sketch_in[far, :]).reshape(DP, 16, R)

    stage[...] = local[...].astype(BF16)

    def stage_copy(k):
        to = (dp + k) % DP
        return send(stage.at[to], landed.at[k - 1], ss.at[k - 1], sr.at[k - 1], {"dp": to})

    to_ring(stage_copy)

    def add(k, total):
        stage_copy(k).wait_recv()
        return total + landed[k - 1].astype(F32)

    own = lax.fori_loop(1, DP, add, local[dp]).astype(BF16)
    sketch[dp] = own
    slots[chip, core] = own

    def sketch_copy(k):
        return send(
            sketch.at[dp], sketch.at[dp], gs.at[k - 1], gr.at[k - 1], {"dp": (dp + k) % DP}
        )

    to_ring(sketch_copy)
    slot_gather = plane_gather(slots.at[chip, core], ps, pr)
    slot_half = slots.at[:, core]
    slot_swap = send(slot_half, slot_half, slot_pair.at[0], slot_pair.at[1], partner)
    wait_all(sketch_copy, 1, DP)
    rows_block = sketch[...].reshape(256, R)

    def raw_half(h):
        return jnp.dot(act[half_rows(h), :], rows_block, preferred_element_type=F32)

    def gram_half(h):
        return gram_local[half_rows(h, PACKED // 2), :]

    sum_raw = PlaneSum(raw_half, raw, BF16, sums[1])
    sum_gram = PlaneSum(gram_half, gram, F32, sums[2])
    sum_raw.start()
    for i in range(LEAVES):
        row = dot_t(rows_block[:, i * LEAF : (i + 1) * LEAF], rows_block[:, i * LEAF :])
        for j in range(i, LEAVES):
            at = UPPER.index((i, j)) * LEAF
            gram_local[at : at + LEAF, :] = row[:, (j - i) * LEAF : (j - i + 1) * LEAF]
    sum_gram.start()
    sum_raw.scatter()
    sum_gram.scatter()
    sum_raw.gather()
    sum_gram.gather()
    sum_raw.share()
    wait_all(slot_gather, 1, CHIPS)
    slot_swap.start()
    sum_raw.end()

    terms[:width, :] = jnp.dot(ogt[...], raw[...], preferred_element_type=F32)

    def terms_of(columns):
        def block(b):
            if isinstance(b, int):
                return terms[b * SLICE : (b + 1) * SLICE, columns]
            return terms[pl.ds(pl.multiple_of(b * SLICE, SLICE), SLICE), columns]

        return block

    fold_one = FoldedScatter(terms_of(slice(0, FIRST)), fold_refs[0])
    fold_two = FoldedScatter(terms_of(slice(FIRST, R)), fold_refs[1])
    fold_one.start()
    sum_gram.share()
    fold_two.start()
    sum_gram.end()
    for n, (i, j) in enumerate(UPPER):
        work[i * LEAF : (i + 1) * LEAF, j * LEAF : (j + 1) * LEAF] = gram[n * LEAF : (n + 1) * LEAF, :]

    def adam(owners, result, whole):
        count = owners.stop - owners.start
        by_owner = result.reshape(count, 2, 16, SLICE)
        packed = jnp.concatenate([by_owner[:, 0], by_owner[:, 1]], axis=2)
        projected[owners] = packed.astype(BF16)
        both = moved[owners].astype(F32).reshape(count * 32, 2 * SLICE)
        new_m = beta_one * both[:, :SLICE] + (1.0 - beta_one) * result
        new_v = beta_two * both[:, SLICE:] + (1.0 - beta_two) * result * result
        correct_one = 1.0 - beta_one**STEP
        correct_two = 1.0 - beta_two**STEP
        direction = new_m / correct_one / (jnp.sqrt(new_v / correct_two) + adam_eps)
        whole[dp] = direction.T.astype(BF16)
        return jnp.sum(direction * direction, keepdims=True)

    gather_one = FoldedGather(whole_one, gather_refs[0])
    gather_two = FoldedGather(whole_two, gather_refs[1])
    by_columns = (((1,), (1,)), ((), ()))

    def basis_columns(k):
        here, after = k * LEAF, (k + 1) * LEAF
        inverse = work[here:after, R : R + after]
        high = inverse.astype(BF16)
        low = (inverse - high.astype(F32)).astype(BF16)
        rows = slots[...].reshape(R, R)[:, :after]
        columns = lax.dot_general(rows, high, by_columns, preferred_element_type=F32)
        columns += lax.dot_general(rows, low, by_columns, preferred_element_type=F32)
        rows_of[:, here:after] = columns.astype(BF16)

    def ring_copy(k):
        to = {"dp": (dp + k) % DP}
        return send(tiles.at[0], squares_in.at[15 + k], zs.at[k - 1], zr.at[k - 1], to)

    pair_copy = send(tiles.at[1], squares_in.at[0], sq_pair.at[0], sq_pair.at[1], partner)

    def chip_copy(k):
        to = {"mp": chip_at(chip, k) * 2 + core}
        return send(tiles.at[2], squares_in.at[k], qs.at[k - 1], qr.at[k - 1], to)

    def back_copy(k):
        to = (dp + k) % DP
        return send(projected.at[to], back.at[dp], bs.at[k - 1], br.at[k - 1], {"dp": to})

    def back_start(h):
        def go(k, _):
            @pl.when((dp + k) % DP // AHEAD == h)
            def _():
                back_copy(k).start()

            return 0

        lax.fori_loop(1, DP, go, 0)

    def add_all(copy, base, total):
        def go(k, value):
            copy(k).wait_recv()
            return value + squares_in[base + k]

        return lax.fori_loop(1, 16, go, total)

    eliminate(work, 0)
    fold_one.fold()
    eliminate(work, 1)
    fold_two.fold()
    eliminate(work, 2)
    slot_swap.wait_recv()
    for k in range(LEAVES - 1):
        basis_columns(k)
    for plane in (sum_in, sum_raw, sum_gram):
        plane.drain()
    slot_swap.wait_send()
    wait_all(slot_gather, 1, CHIPS, recv=False)
    for copy in (stage_copy, sketch_copy, moment_copy):
        wait_all(copy, 1, DP, recv=False)
    wait_all(moment_copy, 1, DP)
    part_one = fold_one.end()
    result = exact_dot(work[:FIRST, R : R + FIRST], part_one, ((1,), (1,)))
    squares = adam(slice(0, AHEAD), result, whole_one)
    gather_one.start()
    back_start(0)
    eliminate(work, LEAVES - 1)
    basis_columns(LEAVES - 1)
    result = exact_dot(work[FIRST:, R : R + FIRST], part_one, ((1,), (1,)))
    part_two = fold_two.end()
    result += exact_dot(work[FIRST:, R + FIRST :], part_two, ((1,), (1,)))
    squares += adam(slice(AHEAD, DP), result, whole_two)
    tiles[0] = jnp.broadcast_to(squares, (1, 128))
    to_ring(ring_copy)
    gather_two.start()
    back_start(1)
    back[dp] = projected[dp]
    gather_one.forward()
    fold_one.drain()
    fold_two.drain()
    tiles[1] = add_all(ring_copy, 15, tiles[0])
    pair_copy.start()
    gather_two.forward()
    pair_copy.wait_recv()
    tiles[2] = tiles[1] + squares_in[0]

    def chip_start(k, _):
        chip_copy(k).start()
        return 0

    lax.fori_loop(1, CHIPS, chip_start, 0)
    gather_one.end()

    def product_of(columns, whole):
        return lax.dot_general(
            rows_of[:, columns],
            whole[...].reshape(WIDE, whole.shape[2]),
            by_columns,
            preferred_element_type=F32,
        )

    product = product_of(slice(0, FIRST), whole_one)
    wait_all(back_copy, 1, DP)
    for r in range(2):
        rows = [back[i, :, r * SLICE : (r + 1) * SLICE].astype(F32) for i in range(DP)]
        sums_out[16 * r : 16 * r + 16, :] = jnp.concatenate(rows, axis=1)[:, :width]
    total_squares = add_all(chip_copy, 0, tiles[2])
    factor = lax.rsqrt(total_squares / (R * FF) + norm_eps)[0:1, 0:1]
    for copy in (ring_copy, back_copy, chip_copy):
        wait_all(copy, 1, 16, recv=False)
    pair_copy.wait_send()
    gather_one.drain()
    gather_two.end()
    product += product_of(slice(FIRST, R), whole_two)
    update[...] = (factor * product[:, :width]).astype(BF16)
    gather_two.drain()


def galore_call(out_grads, test_matrix, activations, first, second):
    return pl.pallas_call(
        galore_kernel,
        out_shape=(
            jax.ShapeDtypeStruct((R, first.shape[1]), BF16),
            jax.ShapeDtypeStruct(first.shape, F32),
        ),
        in_specs=[pl.BlockSpec(memory_space=pltpu.HBM)] * 5,
        out_specs=(VMEM,) * 2,
        scratch_shapes=[
            *PlaneSum.scratch(BF16),
            *PlaneSum.scratch(BF16),
            *PlaneSum.scratch(F32, PACKED // 2, LEAF),
            *FoldedScatter.scratch(SLICE, FIRST),
            *FoldedScatter.scratch(SLICE, R - FIRST),
            *FoldedGather.scratch(),
            *FoldedGather.scratch(),
            pltpu.VMEM((R, R), BF16),
            pltpu.VMEM((DP, 16, R), F32),
            pltpu.VMEM((PACKED, LEAF), F32),
            pltpu.VMEM((PACKED, LEAF), F32),
            pltpu.VMEM((R, R), BF16),
            pltpu.VMEM((WIDE, R), F32),
            pltpu.VMEM((DP, 32, 2 * SLICE), BF16),
            pltpu.VMEM((DP, 32, 2 * SLICE), BF16),
            pltpu.VMEM((DP, 16, R), BF16),
            pltpu.VMEM((DP - 1, 16, R), BF16),
            pltpu.VMEM((DP, 16, R), BF16),
            pltpu.VMEM((CHIPS, 2, 16, R), BF16),
            pltpu.VMEM((R, R), BF16),
            pltpu.VMEM((R, 2 * R), F32),
            pltpu.VMEM((DP, 16, 2 * SLICE), BF16),
            pltpu.VMEM((DP, SLICE, FIRST), BF16),
            pltpu.VMEM((DP, SLICE, R - FIRST), BF16),
            pltpu.VMEM((DP, 16, 2 * SLICE), BF16),
            pltpu.VMEM((3, 1, 128), F32),
            pltpu.VMEM((31, 1, 128), F32),
            *[sem for _ in range(7) for sem in dp_semaphores()],
            pltpu.SemaphoreType.DMA((2,)),
            pltpu.SemaphoreType.DMA((2,)),
            pltpu.VMEM(out_grads.shape[::-1], BF16),
            pltpu.VMEM(test_matrix.shape, BF16),
            pltpu.VMEM(activations.shape, BF16),
            pltpu.VMEM(first.shape, F32),
            pltpu.VMEM(second.shape, F32),
            pltpu.SemaphoreType.DMA((5,)),
        ],
        compiler_params=pltpu.CompilerParams(
            collective_id=0, has_side_effects=True, vmem_limit_bytes=48 * 2**20
        ),
        name="galore_step",
    )(*(pltpu.with_memory_space_constraint(x, pltpu.HBM) for x in (out_grads.T, test_matrix, activations, first, second)))


def shards(activations, out_grads, test_matrix, first_moment, second_moment):
    update, projected = galore_call(
        out_grads, test_matrix, activations, first_moment, second_moment
    )
    new_first = beta_one * first_moment + (1.0 - beta_one) * projected
    new_second = beta_two * second_moment + (1.0 - beta_two) * projected * projected
    return (update.reshape(lax.axis_size("mp"), 16, out_grads.shape[1]), new_first, new_second)


def solution(mesh):
    placed = (P("dp", "mp"), P("dp", "mp"), P("mp", None), P("dp", "mp"), P("dp", "mp"))
    return jax.shard_map(
        shards,
        mesh=mesh,
        in_specs=placed,
        out_specs=(P(None, "dp", "mp"), P("dp", "mp"), P("dp", "mp")),
        check_vma=False,
    )
```

```python
import jax
import jax.numpy as jnp
from jax import lax
from jax.experimental import pallas as pl
from jax.experimental.pallas import tpu as pltpu
from jax.sharding import PartitionSpec as P

FF = 29568
R = 512
STEP = 100

beta_one = 0.9
beta_two = 0.999
adam_eps = 1e-08
norm_eps = 1e-06

MESH = pl.DeviceIdType.MESH
F32 = jnp.float32
BF16 = jnp.bfloat16
CHIPS = 16
DP = 16


def place():
    mp = lax.axis_index("mp")
    core = mp % 2
    chip = mp // 2
    return lax.axis_index("dp"), mp, chip, core


def chip_at(chip, k):
    x = (chip // 4 + k // 4) % 4
    y = (chip % 4 + k % 4) % 4
    return x * 4 + y


def greet(dp_offsets):
    dp, mp, chip, core = place()
    barrier = pltpu.get_barrier_semaphore()
    pl.semaphore_signal(barrier, inc=1, device_id={"mp": chip * 2 + 1 - core}, device_id_type=MESH)

    def to_chip(k, _):
        pl.semaphore_signal(
            barrier, inc=1, device_id={"mp": chip_at(chip, k) * 2 + core}, device_id_type=MESH
        )
        return 0

    lax.fori_loop(1, CHIPS, to_chip, 0)

    def to_ring(k, _):
        pl.semaphore_signal(barrier, inc=1, device_id={"dp": (dp + k) % DP}, device_id_type=MESH)
        return 0

    if dp_offsets == "all":
        lax.fori_loop(1, DP, to_ring, 0)
        return barrier, 1 + (CHIPS - 1) + (DP - 1)
    to_ring(1, 0)
    to_ring(DP - 1, 0)
    return barrier, 1 + (CHIPS - 1) + 2


def send(src, dst, sends, recvs, where):
    return pltpu.make_async_remote_copy(
        src_ref=src, dst_ref=dst, send_sem=sends, recv_sem=recvs, device_id=where, device_id_type=MESH
    )


def to_plane(copy_to):
    def go(i, _):
        copy_to(1 + (9 + i) % 15).start()
        return 0

    lax.fori_loop(0, CHIPS - 1, go, 0)


def plane_scatter(stage, landed, sends, recvs):
    _, _, chip, core = place()

    def copy(k):
        there = chip_at(chip, k)
        return send(
            stage.at[there], landed.at[k - 1], sends.at[k - 1], recvs.at[k - 1], {"mp": there * 2 + core}
        )

    to_plane(copy)
    return copy


def plane_gather(block, sends, recvs):
    _, _, chip, core = place()

    def copy(k):
        there = chip_at(chip, k)
        return send(block, block, sends.at[k - 1], recvs.at[k - 1], {"mp": there * 2 + core})

    to_plane(copy)
    return copy


def wait_all(copy, first, last, recv=True):
    def step(k, _):
        if recv:
            copy(k).wait_recv()
        else:
            copy(k).wait_send()
        return 0

    lax.fori_loop(first, last, step, 0)


class PlaneSum:
    COUNT = 9

    def scratch(kind, half=256, width=R):
        return [
            pltpu.VMEM((half, width), kind),
            pltpu.VMEM((half, width), kind),
            pltpu.VMEM((CHIPS, half // CHIPS, width), kind),
            pltpu.VMEM((CHIPS - 1, half // CHIPS, width), kind),
            pltpu.SemaphoreType.DMA((4,)),
            pltpu.SemaphoreType.DMA((CHIPS - 1,)),
            pltpu.SemaphoreType.DMA((CHIPS - 1,)),
            pltpu.SemaphoreType.DMA((CHIPS - 1,)),
            pltpu.SemaphoreType.DMA((CHIPS - 1,)),
        ]

    def __init__(self, half_of, full, kind, refs):
        self.half_of, self.full, self.kind = half_of, full, kind
        self.give, self.take, self.stage, self.landed, pair, self.s1, self.r1, self.s2, self.r2 = refs
        _, _, self.chip, self.core = place()
        partner = {"mp": self.chip * 2 + 1 - self.core}
        self.swap = send(self.give, self.take, pair.at[0], pair.at[1], partner)
        self.rows = full.shape[0] // 2
        half = full.at[half_rows(self.core, self.rows), :]
        self.swap_full = send(half, half, pair.at[2], pair.at[3], partner)

    def fill(self):
        self.give[...] = self.half_of(1 - self.core).astype(self.kind)

    def start(self):
        self.fill()
        self.swap.start()

    def scatter(self):
        own = self.half_of(self.core)
        self.swap.wait_recv()
        both = own + self.take[...].astype(F32)
        self.stage[...] = both.astype(self.kind).reshape(self.stage.shape)
        self.out = plane_scatter(self.stage, self.landed, self.s1, self.r1)

    def gather(self):
        def add(k, total):
            self.out(k).wait_recv()
            return total + self.landed[k - 1].astype(F32)

        total = lax.fori_loop(1, CHIPS, add, self.stage[self.chip].astype(F32))
        count = self.rows // CHIPS
        mine = pl.ds(pl.multiple_of(self.core * self.rows + self.chip * count, count), count)
        self.full[mine, :] = total.astype(self.kind)
        self.back = plane_gather(self.full.at[mine, :], self.s2, self.r2)

    def share(self):
        wait_all(self.back, 1, CHIPS)
        self.swap_full.start()

    def end(self):
        self.swap_full.wait_recv()

    def drain(self):
        self.swap.wait_send()
        wait_all(self.out, 1, CHIPS, recv=False)
        wait_all(self.back, 1, CHIPS, recv=False)
        self.swap_full.wait_send()


def to_ring(copy_to):
    def go(i, _):
        copy_to(8 + (2 * (i % 2) - 1) * ((i + 1) // 2)).start()
        return 0

    lax.fori_loop(0, DP - 1, go, 0)


class FoldedScatter:
    COUNT = 9

    def scratch(rows, width):
        return [
            pltpu.VMEM((4, 3, rows, width), BF16),
            pltpu.VMEM((4, rows, width), BF16),
            pltpu.VMEM((3, rows, width), BF16),
            pltpu.VMEM((rows, width), F32),
            pltpu.SemaphoreType.DMA((4, 3)),
            pltpu.SemaphoreType.DMA((4, 3)),
            pltpu.SemaphoreType.DMA((3,)),
            pltpu.SemaphoreType.DMA((3,)),
            pltpu.VMEM((DP, rows, width), BF16),
        ]

    def __init__(self, local, refs):
        self.local = local
        self.near, self.stage, self.far, self.own, self.ns, self.nr, self.fs, self.fr, self.give = refs
        self.dp = lax.axis_index("dp")
        self.cls, self.row = self.dp % 4, self.dp // 4

    def near_copy(self, o, j):
        q = (self.row + o) % 4
        step = (1, DP - 1, DP - 2 + 4 * (q % 2))[j]
        to = (self.dp + step) % DP
        return send(
            self.give.at[to % 4 + 4 * q], self.near.at[q, j], self.ns.at[q, j], self.nr.at[q, j], {"dp": to}
        )

    def far_copy(self, o):
        q = (self.row + o) % 4
        return send(
            self.stage.at[q], self.far.at[o - 1], self.fs.at[o - 1], self.fr.at[o - 1],
            {"dp": self.cls + 4 * q},
        )

    def start(self):
        for b in range(DP):
            self.give[b] = self.local(b).astype(BF16)
        for o in (2, 1, 3, 0):
            for j in range(3):
                self.near_copy(o, j).start()

    def fold(self):
        for o in (2, 1, 3, 0):
            q = (self.row + o) % 4
            total = self.local(self.cls + 4 * q)
            for j in range(3):
                self.near_copy(o, j).wait_recv()
                total = total + self.near[q, j].astype(F32)
            if o:
                self.stage[q] = total.astype(BF16)
                self.far_copy(o).start()
            else:
                self.own[...] = total

    def end(self):
        total = self.own[...]
        for o in (1, 3, 2):
            self.far_copy(o).wait_recv()
            total = total + self.far[o - 1].astype(F32)
        return total

    def drain(self):
        for o in range(4):
            for j in range(3):
                self.near_copy(o, j).wait_send()
            if o:
                self.far_copy(o).wait_send()


class FoldedGather:
    COUNT = 4

    def scratch():
        return [
            pltpu.SemaphoreType.DMA((3,)),
            pltpu.SemaphoreType.DMA((3,)),
            pltpu.SemaphoreType.DMA((4, 3)),
            pltpu.SemaphoreType.DMA((4, 3)),
        ]

    def __init__(self, whole, refs):
        self.whole = whole
        self.fs, self.fr, self.ns, self.nr = refs
        self.dp = lax.axis_index("dp")
        self.cls, self.row = self.dp % 4, self.dp // 4

    def far_copy(self, o):
        own = self.whole.at[self.dp]
        to = self.cls + 4 * ((self.row + o) % 4)
        return send(own, own, self.fs.at[o - 1], self.fr.at[o - 1], {"dp": to})

    def near_copy(self, q, j):
        block = self.whole.at[self.cls + 4 * q]
        step = (1, DP - 1, 2 + (DP - 4) * (q % 2))[j]
        return send(
            block, block, self.ns.at[q, j], self.nr.at[q, j], {"dp": (self.dp + step) % DP}
        )

    def start(self):
        for o in (2, 1, 3):
            self.far_copy(o).start()
        for j in range(3):
            self.near_copy(self.row, j).start()

    def forward(self):
        for o in (1, 3, 2):
            self.far_copy(o).wait_recv()
            for j in range(3):
                self.near_copy((self.row + 4 - o) % 4, j).start()

    def end(self):
        for q in range(4):
            for j in range(3):
                self.near_copy(q, j).wait_recv()

    def drain(self):
        for o in range(1, 4):
            self.far_copy(o).wait_send()
        for q in range(4):
            for j in range(3):
                self.near_copy(q, j).wait_send()


def half_rows(h, count=256):
    return pl.ds(pl.multiple_of(h * count, count), count)


def dot_t(a, b):
    return lax.dot_general(a, b, (((0,), (0,)), ((), ())), preferred_element_type=F32)


LEAF = 128


def exact_dot(a, b, dims):
    return lax.dot_general(
        a, b, (dims, ((), ())), precision=lax.Precision.HIGHEST, preferred_element_type=F32
    )


def leaf_inverse(block, inverse):
    groups = LEAF // 8
    sub = lax.broadcasted_iota(jnp.int32, (8, 128), 0)

    def spread(row):
        return jnp.broadcast_to(row, (8, 128))

    for p in range(groups):
        cols = {
            g: [spread(block[g][:, 8 * p + j : 8 * p + j + 1]) for j in range(8)]
            for g in range(p, groups)
        }
        pivots = jnp.zeros((8, 128), F32)
        for j in range(8):
            pivot = spread(cols[p][j][j : j + 1, :])
            over = 1.0 / pivot
            pivots = jnp.where(sub == j, pivot, pivots)
            below = jnp.where(sub > j, cols[p][j], 0.0)
            row_block = spread(block[p][j : j + 1, :]) * over
            row_inverse = spread(inverse[p][j : j + 1, :]) * over
            ratio = {i: spread(cols[p][j][i : i + 1, :]) * over for i in range(j + 1, 8)}
            for g in range(p, groups):
                left = below if g == p else cols[g][j]
                for i in range(j + 1, 8):
                    cols[g][i] = cols[g][i] - left * ratio[i]
                block[g] = block[g] - left * row_block
                inverse[g] = inverse[g] - left * row_inverse
        inverse[p] = inverse[p] * lax.rsqrt(pivots)
    return jnp.concatenate(inverse, axis=0)


VMEM = pl.BlockSpec(memory_space=pltpu.VMEM)


N_PLANE = PlaneSum.COUNT
N_FOLD = FoldedScatter.COUNT
N_GATHER = FoldedGather.COUNT
SLICE = 64
WIDE = DP * SLICE
FIRST = 3 * R // 4
AHEAD = FIRST // 32
LEAVES = R // LEAF
UPPER = [(i, j) for i in range(LEAVES) for j in range(i, LEAVES)]
PACKED = len(UPPER) * LEAF


def dp_semaphores():
    return [pltpu.SemaphoreType.DMA((DP - 1,)) for _ in range(2)]


def eliminate(work, k):
    lane = lax.broadcasted_iota(jnp.int32, (8, 128), 1)
    sub = lax.broadcasted_iota(jnp.int32, (8, 128), 0)
    here, after = k * LEAF, (k + 1) * LEAF
    tail = R - after
    block = [work[here + 8 * g : here + 8 * g + 8, here:after] for g in range(LEAF // 8)]
    unit = [jnp.where(lane == sub + 8 * g, 1.0, 0.0) for g in range(LEAF // 8)]
    inverse = leaf_inverse(block, unit)
    panel = exact_dot(inverse, work[here:after, after : R + here], ((1,), (0,)))
    panel = jnp.concatenate([panel, inverse], axis=1)
    work[here:after, R : R + after] = panel[:, tail:]
    if tail:
        work[after:, after : R + after] -= exact_dot(panel[:, :tail], panel, ((0,), (0,)))


def galore_kernel(ogt_in, tm_in, act_in, first_in, second_in, update, sums_out, *refs):
    sums = [refs[i * N_PLANE : (i + 1) * N_PLANE] for i in range(3)]
    rest = refs[3 * N_PLANE :]
    fold_refs, rest = (rest[:N_FOLD], rest[N_FOLD : 2 * N_FOLD]), rest[2 * N_FOLD :]
    gather_refs, rest = (rest[:N_GATHER], rest[N_GATHER : 2 * N_GATHER]), rest[2 * N_GATHER :]
    sketch_in, local, gram_local, gram, raw, terms, moments, moved, stage, landed, sketch = rest[:11]
    slots, rows_of, work, projected, whole_one, whole_two, back, tiles, squares_in = rest[11:20]
    ms, mr, ss, sr, gs, gr, ps, pr, qs, qr, zs, zr, bs, br, slot_pair, sq_pair = rest[20:36]
    ogt, tm, act, first, second, load_sems = rest[36:]
    dp, mp, chip, core = place()
    partner = {"mp": chip * 2 + 1 - core}
    width = ogt.shape[0]
    pairs = ((ogt_in, ogt), (tm_in, tm), (act_in, act), (first_in, first), (second_in, second))
    loads = [pltpu.make_async_copy(a, b, load_sems.at[i]) for i, (a, b) in enumerate(pairs)]
    for load in loads:
        load.start()
    barrier, count = greet("all")
    loads[0].wait()
    loads[1].wait()

    def in_half(h):
        return dot_t(ogt[:, half_rows(h)], tm[...])

    sum_in = PlaneSum(in_half, sketch_in, BF16, sums[0])
    sum_in.fill()
    loads[3].wait()
    loads[4].wait()
    for i in range(DP):
        stop = min(SLICE, width - i * SLICE)
        if stop < SLICE:
            moments[i] = jnp.zeros((32, 2 * SLICE), BF16)
        if stop > 0:
            moments[i, :, :stop] = first[:, i * SLICE : i * SLICE + stop].astype(BF16)
            moments[i, :, SLICE : SLICE + stop] = second[:, i * SLICE : i * SLICE + stop].astype(BF16)
    pl.semaphore_wait(barrier, count)
    sum_in.swap.start()

    def moment_copy(k):
        to = (dp + k) % DP
        return send(moments.at[to], moved.at[dp], ms.at[k - 1], mr.at[k - 1], {"dp": to})

    to_ring(moment_copy)
    sum_in.scatter()
    moved[dp] = moments[dp]
    sum_in.gather()
    terms[width // 8 * 8 :, :] = jnp.zeros((WIDE - width // 8 * 8, R), F32)
    work[:, R:] = jnp.zeros((R, R), F32)
    sum_in.share()
    loads[2].wait()
    near, far = half_rows(core), half_rows(1 - core)
    local[...] = dot_t(act[near, :], sketch_in[near, :]).reshape(DP, 16, R)
    sum_in.end()
    local[...] += dot_t(act[far, :], sketch_in[far, :]).reshape(DP, 16, R)

    stage[...] = local[...].astype(BF16)

    def stage_copy(k):
        to = (dp + k) % DP
        return send(stage.at[to], landed.at[k - 1], ss.at[k - 1], sr.at[k - 1], {"dp": to})

    to_ring(stage_copy)

    def add(k, total):
        stage_copy(k).wait_recv()
        return total + landed[k - 1].astype(F32)

    own = lax.fori_loop(1, DP, add, local[dp]).astype(BF16)
    sketch[dp] = own
    slots[chip, core] = own

    def sketch_copy(k):
        return send(
            sketch.at[dp], sketch.at[dp], gs.at[k - 1], gr.at[k - 1], {"dp": (dp + k) % DP}
        )

    to_ring(sketch_copy)
    slot_gather = plane_gather(slots.at[chip, core], ps, pr)
    slot_half = slots.at[:, core]
    slot_swap = send(slot_half, slot_half, slot_pair.at[0], slot_pair.at[1], partner)
    wait_all(sketch_copy, 1, DP)
    rows_block = sketch[...].reshape(256, R)

    def raw_half(h):
        return jnp.dot(act[half_rows(h), :], rows_block, preferred_element_type=F32)

    def gram_half(h):
        return gram_local[half_rows(h, PACKED // 2), :]

    sum_raw = PlaneSum(raw_half, raw, BF16, sums[1])
    sum_gram = PlaneSum(gram_half, gram, F32, sums[2])
    sum_raw.start()
    for i in range(LEAVES):
        row = dot_t(rows_block[:, i * LEAF : (i + 1) * LEAF], rows_block[:, i * LEAF :])
        for j in range(i, LEAVES):
            at = UPPER.index((i, j)) * LEAF
            gram_local[at : at + LEAF, :] = row[:, (j - i) * LEAF : (j - i + 1) * LEAF]
    sum_gram.start()
    sum_raw.scatter()
    sum_gram.scatter()
    sum_raw.gather()
    sum_gram.gather()
    sum_raw.share()
    wait_all(slot_gather, 1, CHIPS)
    slot_swap.start()
    sum_raw.end()

    terms[:width, :] = jnp.dot(ogt[...], raw[...], preferred_element_type=F32)

    def terms_of(columns):
        def block(b):
            if isinstance(b, int):
                return terms[b * SLICE : (b + 1) * SLICE, columns]
            return terms[pl.ds(pl.multiple_of(b * SLICE, SLICE), SLICE), columns]

        return block

    fold_one = FoldedScatter(terms_of(slice(0, FIRST)), fold_refs[0])
    fold_two = FoldedScatter(terms_of(slice(FIRST, R)), fold_refs[1])
    fold_one.start()
    sum_gram.share()
    fold_two.start()
    sum_gram.end()
    for n, (i, j) in enumerate(UPPER):
        work[i * LEAF : (i + 1) * LEAF, j * LEAF : (j + 1) * LEAF] = gram[n * LEAF : (n + 1) * LEAF, :]

    def adam(owners, result, whole):
        count = owners.stop - owners.start
        by_owner = result.reshape(count, 2, 16, SLICE)
        packed = jnp.concatenate([by_owner[:, 0], by_owner[:, 1]], axis=2)
        projected[owners] = packed.astype(BF16)
        both = moved[owners].astype(F32).reshape(count * 32, 2 * SLICE)
        new_m = beta_one * both[:, :SLICE] + (1.0 - beta_one) * result
        new_v = beta_two * both[:, SLICE:] + (1.0 - beta_two) * result * result
        correct_one = 1.0 - beta_one**STEP
        correct_two = 1.0 - beta_two**STEP
        direction = new_m / correct_one / (jnp.sqrt(new_v / correct_two) + adam_eps)
        whole[dp] = direction.T.astype(BF16)
        return jnp.sum(direction * direction, keepdims=True)

    gather_one = FoldedGather(whole_one, gather_refs[0])
    gather_two = FoldedGather(whole_two, gather_refs[1])
    by_columns = (((1,), (1,)), ((), ()))

    def basis_columns(k):
        here, after = k * LEAF, (k + 1) * LEAF
        inverse = work[here:after, R : R + after]
        high = inverse.astype(BF16)
        low = (inverse - high.astype(F32)).astype(BF16)
        rows = slots[...].reshape(R, R)[:, :after]
        columns = lax.dot_general(rows, high, by_columns, preferred_element_type=F32)
        columns += lax.dot_general(rows, low, by_columns, preferred_element_type=F32)
        rows_of[:, here:after] = columns.astype(BF16)

    def ring_copy(k):
        to = {"dp": (dp + k) % DP}
        return send(tiles.at[0], squares_in.at[15 + k], zs.at[k - 1], zr.at[k - 1], to)

    pair_copy = send(tiles.at[1], squares_in.at[0], sq_pair.at[0], sq_pair.at[1], partner)

    def chip_copy(k):
        to = {"mp": chip_at(chip, k) * 2 + core}
        return send(tiles.at[2], squares_in.at[k], qs.at[k - 1], qr.at[k - 1], to)

    def back_copy(k):
        to = (dp + k) % DP
        return send(projected.at[to], back.at[dp], bs.at[k - 1], br.at[k - 1], {"dp": to})

    def back_start(h):
        def go(k, _):
            @pl.when((dp + k) % DP // AHEAD == h)
            def _():
                back_copy(k).start()

            return 0

        lax.fori_loop(1, DP, go, 0)

    def add_all(copy, base, total):
        def go(k, value):
            copy(k).wait_recv()
            return value + squares_in[base + k]

        return lax.fori_loop(1, 16, go, total)

    eliminate(work, 0)
    fold_one.fold()
    eliminate(work, 1)
    fold_two.fold()
    eliminate(work, 2)
    slot_swap.wait_recv()
    for k in range(LEAVES - 1):
        basis_columns(k)
    for plane in (sum_in, sum_raw, sum_gram):
        plane.drain()
    slot_swap.wait_send()
    wait_all(slot_gather, 1, CHIPS, recv=False)
    for copy in (stage_copy, sketch_copy, moment_copy):
        wait_all(copy, 1, DP, recv=False)
    wait_all(moment_copy, 1, DP)
    part_one = fold_one.end()
    result = exact_dot(work[:FIRST, R : R + FIRST], part_one, ((1,), (1,)))
    squares = adam(slice(0, AHEAD), result, whole_one)
    gather_one.start()
    back_start(0)
    eliminate(work, LEAVES - 1)
    basis_columns(LEAVES - 1)
    result = exact_dot(work[FIRST:, R : R + FIRST], part_one, ((1,), (1,)))
    part_two = fold_two.end()
    result += exact_dot(work[FIRST:, R + FIRST :], part_two, ((1,), (1,)))
    squares += adam(slice(AHEAD, DP), result, whole_two)
    tiles[0] = jnp.broadcast_to(squares, (1, 128))
    to_ring(ring_copy)
    gather_two.start()
    back_start(1)
    back[dp] = projected[dp]
    gather_one.forward()
    fold_one.drain()
    fold_two.drain()
    tiles[1] = add_all(ring_copy, 15, tiles[0])
    pair_copy.start()
    gather_two.forward()
    pair_copy.wait_recv()
    tiles[2] = tiles[1] + squares_in[0]

    to_plane(chip_copy)
    gather_one.end()

    def product_of(columns, whole):
        return lax.dot_general(
            rows_of[:, columns],
            whole[...].reshape(WIDE, whole.shape[2]),
            by_columns,
            preferred_element_type=F32,
        )

    product = product_of(slice(0, FIRST), whole_one)
    wait_all(back_copy, 1, DP)
    for r in range(2):
        rows = [back[i, :, r * SLICE : (r + 1) * SLICE].astype(F32) for i in range(DP)]
        sums_out[16 * r : 16 * r + 16, :] = jnp.concatenate(rows, axis=1)[:, :width]
    total_squares = add_all(chip_copy, 0, tiles[2])
    factor = lax.rsqrt(total_squares / (R * FF) + norm_eps)[0:1, 0:1]
    for copy in (ring_copy, back_copy, chip_copy):
        wait_all(copy, 1, 16, recv=False)
    pair_copy.wait_send()
    gather_one.drain()
    gather_two.end()
    product += product_of(slice(FIRST, R), whole_two)
    update[...] = (factor * product[:, :width]).astype(BF16)
    gather_two.drain()


def galore_call(out_grads, test_matrix, activations, first, second):
    return pl.pallas_call(
        galore_kernel,
        out_shape=(
            jax.ShapeDtypeStruct((R, first.shape[1]), BF16),
            jax.ShapeDtypeStruct(first.shape, F32),
        ),
        in_specs=[pl.BlockSpec(memory_space=pltpu.HBM)] * 5,
        out_specs=(VMEM,) * 2,
        scratch_shapes=[
            *PlaneSum.scratch(BF16),
            *PlaneSum.scratch(BF16),
            *PlaneSum.scratch(F32, PACKED // 2, LEAF),
            *FoldedScatter.scratch(SLICE, FIRST),
            *FoldedScatter.scratch(SLICE, R - FIRST),
            *FoldedGather.scratch(),
            *FoldedGather.scratch(),
            pltpu.VMEM((R, R), BF16),
            pltpu.VMEM((DP, 16, R), F32),
            pltpu.VMEM((PACKED, LEAF), F32),
            pltpu.VMEM((PACKED, LEAF), F32),
            pltpu.VMEM((R, R), BF16),
            pltpu.VMEM((WIDE, R), F32),
            pltpu.VMEM((DP, 32, 2 * SLICE), BF16),
            pltpu.VMEM((DP, 32, 2 * SLICE), BF16),
            pltpu.VMEM((DP, 16, R), BF16),
            pltpu.VMEM((DP - 1, 16, R), BF16),
            pltpu.VMEM((DP, 16, R), BF16),
            pltpu.VMEM((CHIPS, 2, 16, R), BF16),
            pltpu.VMEM((R, R), BF16),
            pltpu.VMEM((R, 2 * R), F32),
            pltpu.VMEM((DP, 16, 2 * SLICE), BF16),
            pltpu.VMEM((DP, SLICE, FIRST), BF16),
            pltpu.VMEM((DP, SLICE, R - FIRST), BF16),
            pltpu.VMEM((DP, 16, 2 * SLICE), BF16),
            pltpu.VMEM((3, 1, 128), F32),
            pltpu.VMEM((31, 1, 128), F32),
            *[sem for _ in range(7) for sem in dp_semaphores()],
            pltpu.SemaphoreType.DMA((2,)),
            pltpu.SemaphoreType.DMA((2,)),
            pltpu.VMEM(out_grads.shape[::-1], BF16),
            pltpu.VMEM(test_matrix.shape, BF16),
            pltpu.VMEM(activations.shape, BF16),
            pltpu.VMEM(first.shape, F32),
            pltpu.VMEM(second.shape, F32),
            pltpu.SemaphoreType.DMA((5,)),
        ],
        compiler_params=pltpu.CompilerParams(
            collective_id=0, has_side_effects=True, vmem_limit_bytes=48 * 2**20
        ),
        name="galore_step",
    )(*(pltpu.with_memory_space_constraint(x, pltpu.HBM) for x in (out_grads.T, test_matrix, activations, first, second)))


def shards(activations, out_grads, test_matrix, first_moment, second_moment):
    update, projected = galore_call(
        out_grads, test_matrix, activations, first_moment, second_moment
    )
    new_first = beta_one * first_moment + (1.0 - beta_one) * projected
    new_second = beta_two * second_moment + (1.0 - beta_two) * projected * projected
    return (update.reshape(lax.axis_size("mp"), 16, out_grads.shape[1]), new_first, new_second)


def solution(mesh):
    placed = (P("dp", "mp"), P("dp", "mp"), P("mp", None), P("dp", "mp"), P("dp", "mp"))
    return jax.shard_map(
        shards,
        mesh=mesh,
        in_specs=placed,
        out_specs=(P(None, "dp", "mp"), P("dp", "mp"), P("dp", "mp")),
        check_vma=False,
    )
```
